128 devices in a mesh: blank: 8 (over z, core), tool: 16 (over x, y).
Axes of the slice: x: 4, y: 4, z: 4, core: 2. Of those that a mesh axis runs over, the one named last changes fastest.
Arguments:
- tool_temp: float32 [128, 512, 1024], P('tool', 'blank'), may hold values from -6 to 6
- material: int32 [128, 512, 1024], P('tool', 'blank'), may hold values from 0 to 7
- conductivity: float32 [8], replicated, may hold values from 0.15 to 1.3
- shell_temp: float32 [65536, 128], P(('blank', 'tool')), may hold values from -6 to 6
- base_rate: float32 [65536, 128], P(('blank', 'tool')), may hold values from 0.1 to 1
- film: float32 [65536, 128], P(('blank', 'tool')), may hold values from 0.2 to 2
- contact_temp: float32 [65536, 128], P(('blank', 'tool')), may hold values from -6 to 6
- pair_slab: int32 [65536, 1], P(('blank', 'tool')), may hold values from 0 to 15; in each aligned block of 512 rows (0 to 511, 512 to 1023, ...) at most 64 rows name the same one
- pair_block: int32 [65536], P(('blank', 'tool')), may hold values from 0 to 4095
- bead_ids: int32 [524288], P(('blank', 'tool')), may hold values from 0 to 65535
- bead_gain: float32 [524288], P(('blank', 'tool')), may hold values from 0.5 to 2
Outputs:
- tool_out: float32 [128, 512, 1024], P('tool', 'blank')
- shell_out: float32 [65536, 128], P(('blank', 'tool'))
- contact_out: float32 [65536, 128], P(('blank', 'tool'))
The draws below stay inside these ranges and needn't reach their ends.
Inputs may be any that keep to these rules, and one draw needn't show every extreme that they name: `pair_slab`: in the 512 rows of one device no slab is named more than 64 times, a bound that some block reaches.
All inputs are finite; a program needn't handle non-finite values.
Results may differ from the reference program's by a relative error of at most 0.00002.
Values sent between devices are 32-bit elements; how exact they have to be, the bound alone decides.
A program may use at most 192 MiB of HBM per device.

```python
import math
import jax
import jax.numpy as jnp
import numpy as np
from jax import lax

SX = 8
SY = 64
SZ = 1024
BLK_DEV = 512
BEAD_DEV = 4096
NMAT = 8
STEPS = 2
SWEEPS = 4
CAP = 64
VB = 4096
NX = 128
NY = 512
SHELL_BLOCKS = 65536
BEADS = 524288
N_TOOL = 16


def place_ends(result, stream_key, low, top_value):
    dims = result.shape
    index_at = [jax.random.randint(jax.random.fold_in(stream_key, axis), (), 0, dims[axis]) for axis in range(len(dims))]
    result = result.at[tuple(index_at)].set(low)
    longest = dims.index(max(dims))
    index_at[longest] = (index_at[longest] + 1) % dims[longest]
    return result.at[tuple(index_at)].set(top_value)


def steps_of(rng, extent, shards, smallest, top_value):
    def one(dim, blocks):
        heights = jax.random.uniform(jax.random.fold_in(jax.random.fold_in(rng, 6), dim), (blocks,), jnp.float32, smallest / len(shards), top_value / len(shards))
        return jnp.repeat(jnp.exp(heights), extent[dim] // blocks).reshape((-1,) + (1,) * (len(extent) - dim - 1))

    level = one(*shards[0])
    for cut in shards[1:]:
        level = level * one(*cut)
    return level


def routed_block(key, own, number, rows, count, top, most, lean):
    sequence = jax.random.permutation(key, count)
    crowded, common = load_shares(count, rows * top, most, lean, True), load_shares(count, rows * top, most, lean, False)
    places = jnp.arange(count)

    def named(tallies, offset_by):
        used = int((tallies > 0).sum())
        fixed = max(1, used // 4)
        shifted = fixed + (places - fixed + offset_by * (used - fixed)) % max(1, count - fixed)
        return jnp.zeros((count,), jnp.int32).at[sequence[jnp.where(places < fixed, places, shifted)]].set(jnp.asarray(tallies, jnp.int32))

    tallies = jnp.where(number % 4 == 0, named(crowded, number // 4), named(common, number - number // 4 - 1))
    mixed = jax.random.permutation(jax.random.fold_in(own, 3), count)
    giver, receiver = mixed[0:count // 2 * 2:2], mixed[1:count // 2 * 2:2]
    slack = jnp.minimum(tallies[giver] - 1, most - tallies[receiver]) // 2
    slack = jnp.where((giver == sequence[0]) | (receiver == sequence[0]) | (tallies[receiver] == 0), 0, jnp.maximum(slack, 0))
    shifted = jax.random.randint(jax.random.fold_in(own, 4), (count // 2,), 0, 1 << 20) % (slack + 1)
    tallies = tallies.at[giver].add(-shifted).at[receiver].add(shifted)
    labels = jnp.searchsorted(jnp.cumsum(tallies), jnp.arange(rows * top), side="right").astype(jnp.int32)
    listing = labels.reshape(top, rows).T
    listing = listing[jax.random.permutation(jax.random.fold_in(own, 1), rows)]
    offset_by = jax.random.randint(jax.random.fold_in(own, 2), (rows, 1), 0, top)
    return jnp.take_along_axis(listing, (jnp.arange(top)[None, :] + offset_by) % top, axis=1)


def load_shares(amount, total, limit, slope, full):
    portions = [(1 << 20) // math.isqrt(rank ** slope) + 1 for rank in range(1, amount + 1)]
    largest = limit if full else min(limit, max(-(-total // amount), total * portions[0] // sum(portions)))
    least = 1 if total - largest >= amount - 1 else 0
    given, rest = [largest] + [least] * (amount - 1), total - largest - least * (amount - 1)
    while rest > 0:
        candidates = [i for i in range(1, amount) if given[i] < largest] or [i for i in range(1, amount) if given[i] < limit]
        whole, remaining = sum([portions[i] for i in candidates]), rest
        for i in candidates:
            more = min(limit - given[i], max(1, remaining * portions[i] // whole), rest)
            given[i] = given[i] + more
            rest = rest - more
    return np.array(given)


def bell_draw(own_key, shape, deviation, bound, split=(), held_as=jnp.bfloat16):
    drawn = jax.random.normal(own_key, shape, jnp.float32) * deviation
    if len(split) > 0:
        drawn = steps_of(own_key, shape, split, -0.22, 0.18) * drawn
    return jnp.clip(drawn, min=-bound, max=bound).astype(held_as)


def setup_inputs(seed: int = 0) -> dict:
    streams_of = jax.random.split(jax.random.key(seed), 12)
    tool_temp = bell_draw(streams_of[0], (NX, NY, SZ), 1.0, 6.0, ((0, 16), (1, 8)), jnp.float32)
    material = place_ends(jax.random.randint(streams_of[1], (NX, NY, SZ), 0, NMAT), jax.random.fold_in(streams_of[1], 1), 0, NMAT - 1).astype(jnp.int32)
    conductivity = jnp.clip(jnp.exp(jax.random.uniform(streams_of[2], (NMAT,), jnp.float32, math.log(0.15), math.log(1.3))), 0.15, 1.3)
    shell_temp = bell_draw(streams_of[3], (SHELL_BLOCKS, 128), 1.0, 6.0, ((0, 128),), jnp.float32)
    base_rate = jnp.clip(jnp.exp(math.log(1.0) - 2.3025851 * jax.random.uniform(streams_of[4], (SHELL_BLOCKS, 128), jnp.float32) ** steps_of(streams_of[4], (SHELL_BLOCKS, 128), ((0, 128),), -0.2, 0.2)), 0.1, 1.0)
    film = jnp.clip(jnp.exp(math.log(2.0) - 2.3025851 * jax.random.uniform(streams_of[5], (SHELL_BLOCKS, 128), jnp.float32) ** steps_of(streams_of[5], (SHELL_BLOCKS, 128), ((0, 128),), -0.2, 0.2)), 0.2, 2.0)
    contact_temp = bell_draw(streams_of[6], (SHELL_BLOCKS, 128), 1.0, 6.0, ((0, 128),), jnp.float32)
    pair_slab_keys = jax.random.split(jax.random.fold_in(streams_of[7], 1), SHELL_BLOCKS // BLK_DEV)
    pair_slab_turns = jax.random.permutation(jax.random.fold_in(streams_of[7], 3), SHELL_BLOCKS // BLK_DEV)
    pair_slab = jax.vmap(lambda own, number: routed_block(jax.random.fold_in(streams_of[7], 2), own, number, BLK_DEV, N_TOOL, 1, CAP, 2))(pair_slab_keys, pair_slab_turns).reshape((SHELL_BLOCKS, 1))
    pair_block = place_ends(jax.random.randint(streams_of[8], (SHELL_BLOCKS,), 0, VB), jax.random.fold_in(streams_of[8], 1), 0, VB - 1).astype(jnp.int32)
    bead_ids = place_ends(jax.random.randint(streams_of[9], (BEADS,), 0, BLK_DEV * 128), jax.random.fold_in(streams_of[9], 1), 0, (BLK_DEV * 128) - 1).astype(jnp.int32)
    bead_gain = jnp.clip(jnp.exp(math.log(2.0) - 1.3862944 * jax.random.uniform(streams_of[10], (BEADS,), jnp.float32) ** steps_of(streams_of[10], (BEADS,), ((0, 128),), -0.2, 0.2)), 0.5, 2.0)
    return {"tool_temp": tool_temp, "material": material, "conductivity": conductivity, "shell_temp": shell_temp, "base_rate": base_rate, "film": film, "contact_temp": contact_temp, "pair_slab": pair_slab, "pair_block": pair_block, "bead_ids": bead_ids, "bead_gain": bead_gain}


diffuse_step = 0.12
source_step = 0.25
shell_step = 0.5


def offsets():
    return [(2, 1, 1), (0, 1, 1), (1, 2, 1), (1, 0, 1), (1, 1, 2), (1, 1, 0)]


def window(padded, shift, shape):
    return lax.slice(padded, shift, (shift[0] + shape[0], shift[1] + shape[1], shift[2] + shape[2]))


def sweep(field, kpad, source):
    shape = field.shape
    padded = jnp.pad(field, 1)
    center = kpad[1:-1, 1:-1, 1:-1]
    total = jnp.zeros(shape, jnp.float32)
    for shift in offsets():
        face = 0.5 * (center + window(kpad, shift, shape))
        total = total + face * (window(padded, shift, shape) - field)
    return field + diffuse_step * total + source_step * source


def reference(tool_temp, material, conductivity, shell_temp, base_rate, film, contact_temp, pair_slab, pair_block, bead_ids, bead_gain):
    kfield = jnp.zeros(tool_temp.shape, jnp.float32)
    for mat in range(NMAT):
        kfield = jnp.where(material == mat, conductivity[mat], kfield)
    kpad = jnp.pad(kfield, 1)
    zblocks = SZ // 128
    rows = jnp.arange(SHELL_BLOCKS, dtype=jnp.int32)
    blank_idx = (rows // BLK_DEV) // N_TOOL
    slab = pair_slab[:, 0]
    xl = pair_block // (SY * zblocks)
    yl = (pair_block // zblocks) % SY
    zb = pair_block % zblocks
    start = ((slab * SX + xl) * NY + (blank_idx * SY + yl)) * SZ + zb * 128
    index = start[:, None] + jnp.arange(128, dtype=jnp.int32)[None, :]
    shells_dev = BLK_DEV * 128
    bead_shell = (jnp.arange(BEADS, dtype=jnp.int32) // BEAD_DEV) * shells_dev + bead_ids
    theta = shell_temp
    iface = contact_temp
    field = tool_temp
    for step in range(STEPS):
        flux = film * (iface - theta)
        sigma = 1.0 - 0.4 * jnp.tanh(theta)
        force = bead_gain * sigma.reshape(-1)[bead_shell]
        extra = jnp.zeros((SHELL_BLOCKS * 128,), jnp.float32).at[bead_shell].add(force)
        rate = base_rate + extra.reshape(SHELL_BLOCKS, 128)
        theta = theta + shell_step * (flux + sigma * rate)
        source = jnp.zeros((NX * NY * SZ,), jnp.float32).at[index.reshape(-1)].add(-flux.reshape(-1))
        source = source.reshape(field.shape)
        for sweep_idx in range(SWEEPS):
            field = sweep(field, kpad, source)
        iface = field.reshape(-1)[index]
    return field, theta, iface
```

```python
import functools

import jax
import jax.numpy as jnp
from jax import lax
from jax.experimental import pallas as pl
from jax.experimental.pallas import tpu as pltpu
from jax.sharding import PartitionSpec as P

STEPS = 2
SWEEPS = 4
CAP = 64
LANES = 128
TILE = 8
NZ = 2

diffuse_step = 0.12
source_step = 0.25
shell_step = 0.5
face_step = 0.5 * diffuse_step


def split_pair(x):
    hi = x.astype(jnp.bfloat16)
    lo = (x - hi.astype(jnp.float32)).astype(jnp.bfloat16)
    return hi, lo


def one_hot(mask):
    return jnp.where(mask, 1.0, 0.0).astype(jnp.bfloat16)


def fold_rows(acc):
    for shift in (4, 2, 1):
        acc = acc + pltpu.roll(acc, shift, 0)
    return acc


def column_of(row):
    return jnp.transpose(jnp.broadcast_to(row, (LANES, LANES)))


def kernel(
    dims,
    tool_hbm,
    mat_hbm,
    cond,
    theta0,
    base_rate,
    film,
    contact,
    slab_rows,
    block_rows,
    bead_rows,
    gain_rows,
    tool_out,
    shell_out,
    contact_out,
    F,
    K,
    mat,
    Gx,
    Gy,
    Gz,
    SRC,
    W,
    FG,
    O,
    PM,
    PT,
    XB,
    R,
    A,
    BT,
    acc,
    slot_col,
    lin_col,
    metas,
    metar,
    gidx_v,
    gidx_s,
    ys,
    yr,
    kys,
    kyr,
    msg1s,
    msg1r,
    msg2s,
    msg2r,
    backs,
    backr,
    theta1,
    load_sem,
    out_sem,
    idx_sem,
    xss,
    xrs,
    yss,
    yrs,
    kss,
    krs,
    metass,
    metars,
    m1ss,
    m1rs,
    m2ss,
    m2rs,
    bss,
    brs,
):
    n_tool, n_blank, SX, SY, ZB, BLK, BEADROWS = dims
    slots = n_tool * CAP
    voxel_blocks = SX * SY * ZB
    YT = SY // TILE
    NC = ZB // NZ
    groups = BLK // LANES
    qgroups = slots // LANES
    t = lax.axis_index("tool")
    b = lax.axis_index("blank")
    has_left, has_right = t > 0, t < n_tool - 1
    has_down, has_up = b > 0, b < n_blank - 1

    loads = []
    for zb in range(ZB):
        loads.append(
            pltpu.make_async_copy(
                mat_hbm.at[:, :, pl.ds(zb * LANES, LANES)],
                mat.at[:, zb],
                load_sem.at[1, zb],
            )
        )
    for zb in range(ZB):
        loads.append(
            pltpu.make_async_copy(
                tool_hbm.at[:, :, pl.ds(zb * LANES, LANES)],
                F.at[0, pl.ds(1, SX), 1 + zb, pl.ds(TILE, SY), :],
                load_sem.at[0, zb],
            )
        )
    for copy in loads:
        copy.start()

    barrier = pltpu.get_barrier_semaphore()

    @pl.loop(1, n_tool)
    def _(off):
        pl.semaphore_signal(
            barrier, inc=1, device_id={"tool": lax.rem(t + off, n_tool)}, device_id_type=MESH
        )

    @pl.when(has_down)
    def _():
        pl.semaphore_signal(barrier, inc=1, device_id={"blank": b - 1}, device_id_type=MESH)

    @pl.when(has_up)
    def _():
        pl.semaphore_signal(barrier, inc=1, device_id={"blank": b + 1}, device_id_type=MESH)

    def clear_plane(plane):
        @pl.loop(0, ZB)
        def _(zb):
            zeros = jnp.zeros((SY, LANES), jnp.float32)
            K[plane, zb, pl.ds(TILE, SY), :] = zeros
            F[0, plane, 1 + zb, pl.ds(TILE, SY), :] = zeros
            F[1, plane, 1 + zb, pl.ds(TILE, SY), :] = zeros

    @pl.when(jnp.logical_not(has_left))
    def _():
        clear_plane(0)

    @pl.when(jnp.logical_not(has_right))
    def _():
        clear_plane(SX + 1)

    def clear_rim(side):
        zeros = jnp.zeros((ZB, SX, LANES), jnp.float32)
        yr[0, side] = zeros
        yr[1, side] = zeros
        kyr[side] = zeros

    @pl.when(jnp.logical_not(has_down))
    def _():
        clear_rim(0)

    @pl.when(jnp.logical_not(has_up))
    def _():
        clear_rim(1)

    @pl.loop(1, SX + 1)
    def _(p):
        zeros = jnp.zeros((SY, LANES), jnp.float32)
        for par in range(2):
            F[par, p, 0, pl.ds(TILE, SY), :] = zeros
            F[par, p, ZB + 1, pl.ds(TILE, SY), :] = zeros

    sub8 = lax.broadcasted_iota(jnp.int32, (TILE, LANES), 0)
    lane8 = lax.broadcasted_iota(jnp.int32, (TILE, LANES), 1)

    def row8(ref, g):
        return jnp.broadcast_to(ref[pl.ds(g, 1), :], (TILE, LANES))

    for g in range(groups):
        slot_col[pl.ds(g * LANES, LANES), :] = column_of(slab_rows[pl.ds(g, 1), :])
        blk = block_rows[pl.ds(g, 1), :]
        yl = (blk // ZB) % SY
        lin = ((blk // (ZB * SY)) * ZB + blk % ZB) * SY + yl
        lin_col[pl.ds(g * LANES, LANES), :] = column_of(lin)

    slot_rows = []
    for g in range(groups):
        mine = row8(slab_rows, g)

        def count(i, total, mine=mine, g=g):
            other = slot_col[pl.ds(pl.multiple_of(i * TILE, TILE), TILE), :]
            before = (sub8 + i * TILE) < (lane8 + g * LANES)
            return total + jnp.where((other == mine) & before, 1, 0)

        rank = fold_rows(
            lax.fori_loop(0, (g + 1) * LANES // TILE, count, jnp.zeros((TILE, LANES), jnp.int32))
        )
        slot_rows.append(mine * CAP + rank)
    for g in range(groups):
        slot_col[pl.ds(g * LANES, LANES), :] = column_of(slot_rows[g][0:1])

    @pl.loop(0, slots // LANES)
    def _(i):
        rows = lax.broadcasted_iota(jnp.int32, (LANES, LANES), 0) + i * LANES
        for g in range(groups):
            PM[pl.ds(pl.multiple_of(i * LANES, LANES), LANES), g * LANES : (g + 1) * LANES] = one_hot(
                rows == jnp.broadcast_to(slot_rows[g][0:1], (LANES, LANES))
            )

    @pl.loop(0, qgroups)
    def _(q):
        def part(i, total):
            at = pl.ds(pl.multiple_of(i * 16, 16), 16)
            hit = slot_col[at, :] == (lax.broadcasted_iota(jnp.int32, (16, LANES), 1) + q * LANES)
            PT[at, pl.ds(pl.multiple_of(q * LANES, LANES), LANES)] = one_hot(hit)
            named = jnp.where(hit, lin_col[at, :] + 1, 0)
            return total + named[:TILE] + named[TILE:]

        total = lax.fori_loop(0, BLK // 16, part, jnp.zeros((TILE, LANES), jnp.int32), unroll=4)
        metas[q] = fold_rows(total) - 1

    pl.semaphore_wait(barrier, n_tool - 1 + jnp.where(has_down, 1, 0) + jnp.where(has_up, 1, 0))

    def partner(off):
        return lax.rem(t + off, n_tool)

    def source_of(off):
        return lax.rem(t + n_tool - off, n_tool)

    def meta_copy(d, s):
        return pltpu.make_async_remote_copy(
            src_ref=metas.at[d // 2],
            dst_ref=metar.at[s],
            send_sem=metass.at[d],
            recv_sem=metars.at[s],
            device_id={"tool": d},
            device_id_type=MESH,
        )

    def row_copy(src, dst, ssem, rsem):
        def make(d, s):
            return pltpu.make_async_remote_copy(
                src_ref=src.at[d],
                dst_ref=dst.at[s],
                send_sem=ssem.at[d],
                recv_sem=rsem.at[s],
                device_id={"tool": d},
                device_id_type=MESH,
            )

        return make

    msg1_copy = row_copy(msg1s, msg1r, m1ss, m1rs)
    msg2_copy = row_copy(msg2s, msg2r, m2ss, m2rs)
    back_copy = [
        row_copy(backs.at[k], backr.at[k], bss.at[k], brs.at[k]) for k in range(STEPS)
    ]

    def send_all(make, first, last):
        @pl.loop(first, last)
        def _(off):
            make(partner(off), t).start()

    def wait_arrivals(make):
        @pl.loop(1, n_tool)
        def _(off):
            make(partner(off), source_of(off)).wait_recv()

    def wait_sends(make):
        @pl.loop(1, n_tool)
        def _(off):
            make(partner(off), t).wait_send()

    def x_copy(way, par, c):
        zs = pl.ds(1 + c * NZ, NZ)
        rows = pl.ds(TILE, SY)
        src, dst = (1, SX + 1) if way == 0 else (SX, 0)
        return pltpu.make_async_remote_copy(
            src_ref=F.at[par, src, zs, rows, :],
            dst_ref=F.at[par, dst, zs, rows, :],
            send_sem=xss.at[par, way, c],
            recv_sem=xrs.at[par, way, c],
            device_id={"tool": jnp.where(has_left, t - 1, t + 1) if way == 0 else jnp.where(has_right, t + 1, t - 1)},
            device_id_type=MESH,
        )

    def y_copy(way, par, c):
        zs = pl.ds(c * NZ, NZ)
        return pltpu.make_async_remote_copy(
            src_ref=ys.at[par, way, zs],
            dst_ref=yr.at[par, 1 - way, zs],
            send_sem=yss.at[par, way, c],
            recv_sem=yrs.at[par, way, c],
            device_id={"blank": jnp.where(has_down, b - 1, b + 1) if way == 0 else jnp.where(has_up, b + 1, b - 1)},
            device_id_type=MESH,
        )

    def kx_copy(way):
        rows = pl.ds(TILE, SY)
        src, dst = (1, SX + 1) if way == 0 else (SX, 0)
        return pltpu.make_async_remote_copy(
            src_ref=K.at[src, :, rows, :],
            dst_ref=K.at[dst, :, rows, :],
            send_sem=kss.at[0, way],
            recv_sem=krs.at[0, way],
            device_id={"tool": jnp.where(has_left, t - 1, t + 1) if way == 0 else jnp.where(has_right, t + 1, t - 1)},
            device_id_type=MESH,
        )

    def ky_copy(way):
        return pltpu.make_async_remote_copy(
            src_ref=kys.at[way],
            dst_ref=kyr.at[1 - way],
            send_sem=kss.at[1, way],
            recv_sem=krs.at[1, way],
            device_id={"blank": jnp.where(has_down, b - 1, b + 1) if way == 0 else jnp.where(has_up, b + 1, b - 1)},
            device_id_type=MESH,
        )

    sends_x, sends_y = (has_left, has_right), (has_down, has_up)
    gets_x, gets_y = (has_right, has_left), (has_up, has_down)

    def at_each(flags, act):
        for way in range(2):
            @pl.when(flags[way])
            def _(way=way):
                act(way)

    for zb in range(ZB):
        loads[zb].wait()

    @pl.loop(0, SX)
    def _(xl):
        @pl.loop(0, ZB)
        def _(zb):
            m = mat[xl, zb]
            low, mid, top = (m & 1) != 0, (m & 2) != 0, (m & 4) != 0
            pairs = [jnp.where(low, cond[2 * i + 1], cond[2 * i]) for i in range(4)]
            quads = [jnp.where(mid, pairs[2 * i + 1], pairs[2 * i]) for i in range(2)]
            K[1 + xl, zb, pl.ds(TILE, SY), :] = jnp.where(top, quads[1], quads[0])

    at_each(sends_x, lambda way: kx_copy(way).start())

    @pl.loop(0, ZB)
    def _(zb):
        for xl in range(SX):
            kys[0, zb, pl.ds(xl, 1), :] = K[1 + xl, zb, pl.ds(TILE, 1), :]
            kys[1, zb, pl.ds(xl, 1), :] = K[1 + xl, zb, pl.ds(TILE + SY - 1, 1), :]

    at_each(sends_y, lambda way: ky_copy(way).start())

    outflow = film[...] * (theta0[...] - contact[...])
    hi, lo = split_pair(outflow)
    XB[:, 0:LANES] = hi
    XB[:, LANES : 2 * LANES] = lo
    part_rows = min(512, slots)
    step_rows = min(512, voxel_blocks)

    def pack(write, columns):
        @pl.loop(0, slots // part_rows)
        def _(i):
            got = jnp.dot(
                PM[pl.ds(pl.multiple_of(i * part_rows, part_rows), part_rows), :],
                XB[:, columns : columns + 2 * LANES],
                preferred_element_type=jnp.float32,
            )
            rows = got[:, :LANES] + got[:, LANES:]
            write(i * (part_rows // CAP), rows.reshape(part_rows // CAP, CAP, LANES))

    def write1(d, rows):
        msg1s[pl.ds(d, part_rows // CAP)] = rows

    pack(write1, 0)
    send_all(meta_copy, 1, n_tool)
    send_all(msg1_copy, 1, n_tool)
    metar[t] = metas[t // 2]
    msg1r[t] = msg1s[t]

    def pack_y(par, c):
        for i in range(NZ):
            for xl in range(SX):
                zb = c * NZ + i
                ys[par, 0, zb, pl.ds(xl, 1), :] = F[par, 1 + xl, 1 + zb, pl.ds(TILE, 1), :]
                ys[par, 1, zb, pl.ds(xl, 1), :] = F[par, 1 + xl, 1 + zb, pl.ds(TILE + SY - 1, 1), :]

    def unpack_y(par, c):
        for i in range(NZ):
            for xl in range(SX):
                zb = c * NZ + i
                F[par, 1 + xl, 1 + zb, pl.ds(TILE - 1, 1), :] = yr[par, 0, zb, pl.ds(xl, 1), :]
                F[par, 1 + xl, 1 + zb, pl.ds(TILE + SY, 1), :] = yr[par, 1, zb, pl.ds(xl, 1), :]

    for zb in range(ZB):
        loads[ZB + zb].wait()

    @pl.loop(0, NC)
    def _(c):
        at_each(sends_x, lambda way: x_copy(way, 0, c).start())
        pack_y(0, c)
        at_each(sends_y, lambda way: y_copy(way, 0, c).start())

    for j in range(BEADROWS // TILE):
        @pl.loop(0, TILE)
        def _(i, j=j):
            at = pl.ds(pl.multiple_of(i * LANES, LANES), LANES)
            shell = bead_rows[pl.ds(j * TILE + i, 1), :]
            row, lane = shell // LANES, shell % LANES
            A[:, at] = one_hot(
                lax.broadcasted_iota(jnp.int32, (BLK, LANES), 0) == jnp.broadcast_to(row, (BLK, LANES))
            )
            here = lax.broadcasted_iota(jnp.int32, (LANES, LANES), 0) == jnp.broadcast_to(lane, (LANES, LANES))
            held = jnp.where(here, jnp.broadcast_to(gain_rows[pl.ds(j * TILE + i, 1), :], (LANES, LANES)), 0.0)
            hi, lo = split_pair(held)
            BT[0:LANES, at] = hi
            BT[LANES : 2 * LANES, at] = lo

        part = lax.dot_general(
            A[...], BT[...], (((1,), (1,)), ((), ())), preferred_element_type=jnp.float32
        )
        if j == 0:
            acc[...] = part
        else:
            acc[...] += part

    sigma = 1.0 - 0.4 * jnp.tanh(theta0[...])
    rate = base_rate[...] + sigma * (acc[:, :LANES] + acc[:, LANES:])
    after = theta0[...] + shell_step * (sigma * rate - outflow)
    theta1[...] = after
    hi, lo = split_pair(film[...])
    XB[:, 0:LANES] = hi
    XB[:, LANES : 2 * LANES] = lo
    hi, lo = split_pair(film[...] * after)
    XB[:, 2 * LANES : 3 * LANES] = hi
    XB[:, 3 * LANES : 4 * LANES] = lo

    def write2(d, rows, first):
        msg2s[pl.ds(d, part_rows // CAP), first : first + CAP, :] = rows

    pack(lambda d, rows: write2(d, rows, 0), 0)
    pack(lambda d, rows: write2(d, rows, CAP), 2 * LANES)
    msg2r[t] = msg2s[t]

    lane = lax.broadcasted_iota(jnp.int32, (SY, LANES), 1)
    last_lane, first_lane = lane == LANES - 1, lane == 0

    @pl.loop(0, SX)
    def _(xl):
        here = K[1 + xl, 0, pl.ds(TILE, SY), :]
        turned = pltpu.roll(here, LANES - 1, 1)
        Gz[xl, 0] = face_step * turned
        for zb in range(ZB):
            if zb < ZB - 1:
                after_here = K[1 + xl, zb + 1, pl.ds(TILE, SY), :]
                turned_after = pltpu.roll(after_here, LANES - 1, 1)
                up = jnp.where(last_lane, turned_after, turned)
            else:
                after_here, turned_after = here, turned
                up = jnp.where(last_lane, 0.0, turned)
            Gz[xl, 1 + zb] = face_step * (here + up)
            here, turned = after_here, turned_after

    def x_faces(p):
        @pl.loop(0, ZB)
        def _(zb):
            Gx[p, zb] = face_step * (K[p, zb, pl.ds(TILE, SY), :] + K[p + 1, zb, pl.ds(TILE, SY), :])

    @pl.loop(1, SX)
    def _(p):
        x_faces(p)

    wait_arrivals(meta_copy)
    even = lax.rem(t, 2) == 0
    lin_rows = []
    for q in range(qgroups):
        first, second = metar[2 * q], metar[2 * q + 1]
        first = jnp.where(even, first, pltpu.roll(first, CAP, 1))
        second = jnp.where(even, pltpu.roll(second, CAP, 1), second)
        lin = jnp.where(lane8 < CAP, first, second)
        lin_rows.append(lin)
        gidx_v[pl.ds(q, 1), :] = jnp.maximum(lin[0:1], 0)
    to_smem = pltpu.make_async_copy(gidx_v, gidx_s, idx_sem)
    to_smem.start()

    @pl.loop(0, voxel_blocks // LANES)
    def _(i):
        rows = lax.broadcasted_iota(jnp.int32, (LANES, LANES), 0) + i * LANES
        for q in range(qgroups):
            O[pl.ds(pl.multiple_of(i * LANES, LANES), LANES), q * LANES : (q + 1) * LANES] = one_hot(
                rows == jnp.broadcast_to(lin_rows[q][0:1], (LANES, LANES))
            )

    to_smem.wait()

    at_each(gets_y, lambda way: ky_copy(way).wait_recv())

    @pl.loop(0, ZB)
    def _(zb):
        for xl in range(SX):
            K[1 + xl, zb, pl.ds(TILE - 1, 1), :] = kyr[0, zb, pl.ds(xl, 1), :]
            K[1 + xl, zb, pl.ds(TILE + SY, 1), :] = kyr[1, zb, pl.ds(xl, 1), :]

    @pl.loop(0, SX)
    def _(xl):
        @pl.loop(0, ZB)
        def _(zb):
            Gy[xl, zb, pl.ds(TILE - 1, 1), :] = face_step * (
                K[1 + xl, zb, pl.ds(TILE - 1, 1), :] + K[1 + xl, zb, pl.ds(TILE, 1), :]
            )
            Gy[xl, zb, pl.ds(TILE, SY), :] = face_step * (
                K[1 + xl, zb, pl.ds(TILE, SY), :] + K[1 + xl, zb, pl.ds(TILE + 1, SY), :]
            )

    at_each(gets_x, lambda way: kx_copy(way).wait_recv())
    x_faces(0)
    x_faces(SX)

    def split_rows(src, rows, first, column):
        @pl.loop(0, n_tool)
        def _(s):
            hi, lo = split_pair(src[s, first : first + rows, :])
            at = pl.ds(pl.multiple_of(s * CAP, CAP), CAP)
            R[at, column : column + LANES] = hi
            R[at, column + LANES : column + 2 * LANES] = lo

    def scatter(column, write):
        @pl.loop(0, voxel_blocks // step_rows)
        def _(m):
            at = pl.ds(pl.multiple_of(m * step_rows, step_rows), step_rows)
            got = jnp.dot(
                O[at, :], R[:, column : column + 2 * LANES], preferred_element_type=jnp.float32
            )
            write(at, source_step * (got[:, :LANES] + got[:, LANES:]))

    def to_source(at, rows):
        SRC[at, :] = rows

    def to_weight(at, rows):
        W[at, :] = rows

    wait_arrivals(msg1_copy)
    split_rows(msg1r, CAP, 0, 0)
    scatter(0, to_source)

    lane_t = lax.broadcasted_iota(jnp.int32, (TILE, LANES), 1)
    top_lane, low_lane = lane_t == LANES - 1, lane_t == 0

    def planes(cur, c, yt, first, last):
        new = 1 - cur
        y0 = pl.multiple_of(yt * TILE, TILE)
        rows = pl.ds(pl.multiple_of(y0 + TILE, TILE), TILE)

        def temp(p, i, shift=0):
            if shift:
                return F[cur, p, 1 + c * NZ + i, pl.ds(y0 + TILE + shift, TILE), :]
            return F[cur, p, 1 + c * NZ + i, rows, :]

        def face_x(p, i):
            return Gx[p, c * NZ + i, pl.ds(y0, TILE), :]

        center = [temp(first, i) for i in range(NZ)]
        below = [face_x(first - 1, i) * (center[i] - temp(first - 1, i)) for i in range(NZ)]
        for p in range(first, last):
            xl = p - 1
            ahead = [temp(p + 1, i) for i in range(NZ)]
            above = [face_x(p, i) * (ahead[i] - center[i]) for i in range(NZ)]
            line = [temp(p, -1)] + center + [temp(p, NZ)]
            turned = [None] + [pltpu.roll(line[i], LANES - 1, 1) for i in range(1, NZ + 2)]
            flow = [Gz[xl, c * NZ, pl.ds(y0, TILE), :] * (turned[1] - line[0])]
            for i in range(1, NZ + 1):
                up = jnp.where(top_lane, turned[i + 1], turned[i])
                flow.append(Gz[xl, c * NZ + i, pl.ds(y0, TILE), :] * (up - line[i]))
            moved = [pltpu.roll(flow[i], 1, 1) for i in range(NZ + 1)]
            for i in range(NZ):
                z_part = flow[i + 1] - jnp.where(low_lane, moved[i], moved[i + 1])
                y_high = Gy[xl, c * NZ + i, rows, :] * (temp(p, i, 1) - center[i])
                y_low = Gy[xl, c * NZ + i, pl.ds(y0 + TILE - 1, TILE), :] * (center[i] - temp(p, i, -1))
                at = pl.multiple_of((xl * ZB + c * NZ + i) * SY + y0, TILE)
                total = (above[i] - below[i]) + (y_high - y_low) + z_part
                F[new, p, 1 + c * NZ + i, rows, :] = center[i] + (total + SRC[pl.ds(at, TILE), :])
            center, below = ahead, above

    def keep(cur, with_source):
        @pl.loop(0, SX)
        def _(xl):
            @pl.loop(0, ZB)
            def _(zb):
                at = pl.ds(pl.multiple_of((xl * ZB + zb) * SY, SY), SY)
                now = F[cur, 1 + xl, 1 + zb, pl.ds(TILE, SY), :]
                FG[at, :] = now
                if with_source:
                    SRC[at, :] = SRC[at, :] - W[at, :] * now

    def collect(k):
        @pl.loop(0, n_tool)
        def _(s):
            q = s // 2
            lane0 = lax.rem(s, 2) * CAP

            @pl.loop(0, CAP // TILE)
            def _(j):
                for i in range(TILE):
                    row = gidx_s[q, lane0 + j * TILE + i]
                    backs[k, s, pl.ds(pl.multiple_of(j * TILE, TILE) + i, 1), :] = FG[pl.ds(row, 1), :]

    total_sweeps = STEPS * SWEEPS

    @pl.loop(0, total_sweeps)
    def _(s):
        cur = lax.rem(s, 2)
        new = 1 - cur

        @pl.loop(0, NC)
        def _(c):
            at_each(gets_y, lambda way: y_copy(way, cur, c).wait_recv())
            unpack_y(cur, c)
            at_each(gets_x, lambda way: x_copy(way, cur, c).wait_recv())

            @pl.when(s >= 1)
            def _():
                at_each(sends_x, lambda way: x_copy(way, new, c).wait_send())
                at_each(sends_y, lambda way: y_copy(way, new, c).wait_send())

            @pl.loop(0, YT)
            def _(yt):
                planes(cur, c, yt, 1, 2)
                planes(cur, c, yt, SX, SX + 1)

            @pl.when(s < total_sweeps - 1)
            def _():
                at_each(sends_x, lambda way: x_copy(way, new, c).start())

            @pl.loop(0, YT)
            def _(yt):
                planes(cur, c, yt, 2, SX)

            @pl.when(s < total_sweeps - 1)
            def _():
                pack_y(new, c)
                at_each(sends_y, lambda way: y_copy(way, new, c).start())

        half = (n_tool + 1) // 2

        @pl.when(s == 0)
        def _():
            send_all(msg2_copy, 1, half)

        @pl.when(s == 1)
        def _():
            send_all(msg2_copy, half, n_tool)

        @pl.when(s == 2)
        def _():
            wait_arrivals(msg2_copy)
            split_rows(msg2r, CAP, 0, 0)
            split_rows(msg2r, CAP, CAP, 2 * LANES)
            scatter(0, to_weight)

        @pl.when(s == SWEEPS - 1)
        def _():
            scatter(2 * LANES, to_source)
            keep(new, True)

        @pl.when(s == SWEEPS)
        def _():
            collect(0)
            send_all(back_copy[0], 1, half)

        @pl.when(s == SWEEPS + 1)
        def _():
            send_all(back_copy[0], half, n_tool)

    keep(0, False)
    stores = [
        pltpu.make_async_copy(
            FG.at[pl.ds((xl * ZB + zb) * SY, SY), :],
            tool_out.at[xl, :, pl.ds(zb * LANES, LANES)],
            out_sem.at[xl, zb],
        )
        for xl in range(SX)
        for zb in range(ZB)
    ]
    collect(1)
    send_all(back_copy[1], 1, n_tool)
    for copy in stores:
        copy.start()

    def contact_of(k):
        backr[k, t] = backs[k, t]
        wait_arrivals(back_copy[k])
        split_rows(backr.at[k], CAP, 0, 0)
        got = jnp.dot(PT[...], R[:, 0 : 2 * LANES], preferred_element_type=jnp.float32)
        return got[:, :LANES] + got[:, LANES:]

    flux = film[...] * (contact_of(0) - theta1[...])
    sigma = 1.0 - 0.4 * jnp.tanh(theta1[...])
    rate = base_rate[...] + sigma * (acc[:, :LANES] + acc[:, LANES:])
    shell_out[...] = theta1[...] + shell_step * (flux + sigma * rate)
    contact_out[...] = contact_of(1)

    wait_sends(meta_copy)
    wait_sends(msg1_copy)
    wait_sends(msg2_copy)
    wait_sends(back_copy[0])
    wait_sends(back_copy[1])
    at_each(sends_x, lambda way: kx_copy(way).wait_send())
    at_each(sends_y, lambda way: ky_copy(way).wait_send())

    last = (total_sweeps - 1) % 2

    @pl.loop(0, NC)
    def _(c):
        at_each(sends_x, lambda way: x_copy(way, last, c).wait_send())
        at_each(sends_y, lambda way: y_copy(way, last, c).wait_send())

    for copy in stores:
        copy.wait()


MESH = pl.DeviceIdType.MESH


def on_device(n_tool, n_blank, tool_temp, material, conductivity, shell_temp, base_rate, film, contact_temp, pair_slab, pair_block, bead_ids, bead_gain):
    SX, SY, SZ = tool_temp.shape
    ZB = SZ // LANES
    NC = ZB // NZ
    BLK = shell_temp.shape[0]
    beadrows = bead_ids.shape[0] // LANES
    slots = n_tool * CAP
    voxel_blocks = SX * SY * ZB
    f32, bf16, i32 = jnp.float32, jnp.bfloat16, jnp.int32
    V = pltpu.VMEM
    dma = pltpu.SemaphoreType.DMA
    scratch = [
        V((2, SX + 2, ZB + 2, SY + 2 * TILE, LANES), f32),
        V((SX + 2, ZB, SY + 2 * TILE, LANES), f32),
        V((SX, ZB, SY, LANES), i32),
        V((SX + 1, ZB, SY, LANES), f32),
        V((SX, ZB, SY + TILE, LANES), f32),
        V((SX, ZB + 1, SY, LANES), f32),
        V((voxel_blocks, LANES), f32),
        V((voxel_blocks, LANES), f32),
        V((voxel_blocks, LANES), f32),
        V((voxel_blocks, slots), bf16),
        V((slots, BLK), bf16),
        V((BLK, slots), bf16),
        V((BLK, 4 * LANES), bf16),
        V((slots, 4 * LANES), bf16),
        V((BLK, TILE * LANES), bf16),
        V((2 * LANES, TILE * LANES), bf16),
        V((BLK, 2 * LANES), f32),
        V((BLK, LANES), i32),
        V((BLK, LANES), i32),
        V((slots // LANES, TILE, LANES), i32),
        V((n_tool, TILE, LANES), i32),
        V((slots // LANES, LANES), i32),
        pltpu.SMEM((slots // LANES, LANES), i32),
        V((2, 2, ZB, SX, LANES), f32),
        V((2, 2, ZB, SX, LANES), f32),
        V((2, ZB, SX, LANES), f32),
        V((2, ZB, SX, LANES), f32),
        V((n_tool, CAP, LANES), f32),
        V((n_tool, CAP, LANES), f32),
        V((n_tool, 2 * CAP, LANES), f32),
        V((n_tool, 2 * CAP, LANES), f32),
        V((STEPS, n_tool, CAP, LANES), f32),
        V((STEPS, n_tool, CAP, LANES), f32),
        V((BLK, LANES), f32),
        dma((2, ZB)),
        dma((SX, ZB)),
        dma,
        dma((2, 2, NC)),
        dma((2, 2, NC)),
        dma((2, 2, NC)),
        dma((2, 2, NC)),
        dma((2, 2)),
        dma((2, 2)),
        dma((n_tool,)),
        dma((n_tool,)),
        dma((n_tool,)),
        dma((n_tool,)),
        dma((n_tool,)),
        dma((n_tool,)),
        dma((STEPS, n_tool)),
        dma((STEPS, n_tool)),
    ]
    whole = pl.BlockSpec(memory_space=pltpu.VMEM)
    far = pl.BlockSpec(memory_space=pl.ANY)
    return pl.pallas_call(
        functools.partial(kernel, (n_tool, n_blank, SX, SY, ZB, BLK, beadrows)),
        out_shape=(
            jax.ShapeDtypeStruct(tool_temp.shape, f32),
            jax.ShapeDtypeStruct(shell_temp.shape, f32),
            jax.ShapeDtypeStruct(shell_temp.shape, f32),
        ),
        in_specs=[far, far, pl.BlockSpec(memory_space=pltpu.SMEM)] + [whole] * 8,
        out_specs=(far, whole, whole),
        scratch_shapes=scratch,
        compiler_params=pltpu.CompilerParams(
            collective_id=0, has_side_effects=True, vmem_limit_bytes=60 * 2**20
        ),
    )(
        tool_temp,
        material,
        conductivity,
        shell_temp,
        base_rate,
        film,
        contact_temp,
        pair_slab.reshape(BLK // LANES, LANES),
        pair_block.reshape(BLK // LANES, LANES),
        bead_ids.reshape(beadrows, LANES),
        bead_gain.reshape(beadrows, LANES),
    )


def solution(mesh):
    placed = (
        P("tool", "blank", None),
        P("tool", "blank", None),
        P(),
        P(("blank", "tool"), None),
        P(("blank", "tool"), None),
        P(("blank", "tool"), None),
        P(("blank", "tool"), None),
        P(("blank", "tool"), None),
        P(("blank", "tool")),
        P(("blank", "tool")),
        P(("blank", "tool")),
    )
    return jax.shard_map(
        functools.partial(on_device, mesh.shape["tool"], mesh.shape["blank"]),
        mesh=mesh,
        in_specs=placed,
        out_specs=(
            P("tool", "blank", None),
            P(("blank", "tool"), None),
            P(("blank", "tool"), None),
        ),
        check_vma=False,
    )
```

```python
import functools

import jax
import jax.numpy as jnp
from jax import lax
from jax.experimental import pallas as pl
from jax.experimental.pallas import tpu as pltpu
from jax.sharding import PartitionSpec as P

STEPS = 2
SWEEPS = 4
CAP = 64
LANES = 128
TILE = 8
CHUNKS = 4

diffuse_step = 0.12
source_step = 0.25
shell_step = 0.5
face_step = 0.5 * diffuse_step


def split_pair(x):
    hi = x.astype(jnp.bfloat16)
    lo = (x - hi.astype(jnp.float32)).astype(jnp.bfloat16)
    return hi, lo


def one_hot(mask):
    return jnp.where(mask, 1.0, 0.0).astype(jnp.bfloat16)


def fold_rows(acc):
    for shift in (4, 2, 1):
        acc = acc + pltpu.roll(acc, shift, 0)
    return acc


def column_of(row):
    return jnp.transpose(jnp.broadcast_to(row, (LANES, LANES)))


def kernel(
    dims,
    tool_hbm,
    mat_hbm,
    cond,
    theta0,
    base_rate,
    film,
    contact,
    slab_rows,
    block_rows,
    bead_rows,
    gain_rows,
    tool_out,
    shell_out,
    contact_out,
    FA,
    FB,
    K,
    mat,
    Gx,
    Gy,
    GzH,
    GzL,
    SRC,
    W,
    FG,
    O,
    PM,
    PT,
    XB,
    R,
    A,
    BT,
    acc,
    slot_col,
    lin_col,
    metas,
    metar,
    gidx_v,
    gidx_s,
    ys,
    yr,
    kys,
    kyr,
    msg1s,
    msg1r,
    msg2s,
    msg2r,
    backs,
    backr,
    theta1,
    load_sem,
    out_sem,
    idx_sem,
    xss,
    xrs,
    yss,
    yrs,
    kss,
    krs,
    metass,
    metars,
    m1ss,
    m1rs,
    m2ss,
    m2rs,
    bss,
    brs,
):
    n_tool, n_blank, SX, SY, ZB, BLK, BEADROWS = dims
    slots = n_tool * CAP
    voxel_blocks = SX * SY * ZB
    NC = CHUNKS
    CY = SY // NC
    F = (FA, FB)
    groups = BLK // LANES
    qgroups = slots // LANES
    t = lax.axis_index("tool")
    b = lax.axis_index("blank")
    has_left, has_right = t > 0, t < n_tool - 1
    has_down, has_up = b > 0, b < n_blank - 1

    loads = []
    for zb in range(ZB):
        loads.append(
            pltpu.make_async_copy(
                mat_hbm.at[:, :, pl.ds(zb * LANES, LANES)],
                mat.at[:, zb],
                load_sem.at[1, zb],
            )
        )
    for zb in range(ZB):
        loads.append(
            pltpu.make_async_copy(
                tool_hbm.at[:, :, pl.ds(zb * LANES, LANES)],
                FA.at[pl.ds(1, SX), zb, pl.ds(TILE, SY), :],
                load_sem.at[0, zb],
            )
        )
    for copy in loads:
        copy.start()

    barrier = pltpu.get_barrier_semaphore()

    @pl.loop(1, n_tool)
    def _(off):
        pl.semaphore_signal(
            barrier, inc=1, device_id={"tool": lax.rem(t + off, n_tool)}, device_id_type=MESH
        )

    @pl.when(has_down)
    def _():
        pl.semaphore_signal(barrier, inc=1, device_id={"blank": b - 1}, device_id_type=MESH)

    @pl.when(has_up)
    def _():
        pl.semaphore_signal(barrier, inc=1, device_id={"blank": b + 1}, device_id_type=MESH)

    def clear_plane(plane):
        @pl.loop(0, ZB)
        def _(zb):
            zeros = jnp.zeros((SY, LANES), jnp.float32)
            K[plane, zb, pl.ds(TILE, SY), :] = zeros
            FA[plane, zb, pl.ds(TILE, SY), :] = zeros
            FB[plane, zb, pl.ds(TILE, SY), :] = zeros

    @pl.when(jnp.logical_not(has_left))
    def _():
        clear_plane(0)

    @pl.when(jnp.logical_not(has_right))
    def _():
        clear_plane(SX + 1)

    def clear_rim(side):
        zeros = jnp.zeros((ZB, SX, LANES), jnp.float32)
        yr[0, side] = zeros
        yr[1, side] = zeros
        kyr[side] = zeros

    @pl.when(jnp.logical_not(has_down))
    def _():
        clear_rim(0)

    @pl.when(jnp.logical_not(has_up))
    def _():
        clear_rim(1)

    sub8 = lax.broadcasted_iota(jnp.int32, (TILE, LANES), 0)
    lane8 = lax.broadcasted_iota(jnp.int32, (TILE, LANES), 1)

    def row8(ref, g):
        return jnp.broadcast_to(ref[pl.ds(g, 1), :], (TILE, LANES))

    for g in range(groups):
        slot_col[pl.ds(g * LANES, LANES), :] = column_of(slab_rows[pl.ds(g, 1), :])
        blk = block_rows[pl.ds(g, 1), :]
        yl = (blk // ZB) % SY
        lin = ((blk // (ZB * SY)) * ZB + blk % ZB) * SY + yl
        lin_col[pl.ds(g * LANES, LANES), :] = column_of(lin)

    slot_rows = []
    for g in range(groups):
        mine = row8(slab_rows, g)

        def count(i, total, mine=mine, g=g):
            other = slot_col[pl.ds(pl.multiple_of(i * TILE, TILE), TILE), :]
            before = (sub8 + i * TILE) < (lane8 + g * LANES)
            return total + jnp.where((other == mine) & before, 1, 0)

        rank = fold_rows(
            lax.fori_loop(0, (g + 1) * LANES // TILE, count, jnp.zeros((TILE, LANES), jnp.int32))
        )
        slot_rows.append(mine * CAP + rank)
    for g in range(groups):
        slot_col[pl.ds(g * LANES, LANES), :] = column_of(slot_rows[g][0:1])

    @pl.loop(0, slots // LANES)
    def _(i):
        rows = lax.broadcasted_iota(jnp.int32, (LANES, LANES), 0) + i * LANES
        for g in range(groups):
            PM[pl.ds(pl.multiple_of(i * LANES, LANES), LANES), g * LANES : (g + 1) * LANES] = one_hot(
                rows == jnp.broadcast_to(slot_rows[g][0:1], (LANES, LANES))
            )

    @pl.loop(0, qgroups)
    def _(q):
        def part(i, total):
            at = pl.ds(pl.multiple_of(i * 16, 16), 16)
            hit = slot_col[at, :] == (lax.broadcasted_iota(jnp.int32, (16, LANES), 1) + q * LANES)
            PT[at, pl.ds(pl.multiple_of(q * LANES, LANES), LANES)] = one_hot(hit)
            named = jnp.where(hit, lin_col[at, :] + 1, 0)
            return total + named[:TILE] + named[TILE:]

        total = lax.fori_loop(0, BLK // 16, part, jnp.zeros((TILE, LANES), jnp.int32), unroll=4)
        metas[q] = fold_rows(total) - 1

    pl.semaphore_wait(barrier, n_tool - 1 + jnp.where(has_down, 1, 0) + jnp.where(has_up, 1, 0))

    def partner(off):
        return lax.rem(t + off, n_tool)

    def source_of(off):
        return lax.rem(t + n_tool - off, n_tool)

    def meta_copy(d, s):
        return pltpu.make_async_remote_copy(
            src_ref=metas.at[d // 2],
            dst_ref=metar.at[s],
            send_sem=metass.at[d],
            recv_sem=metars.at[s],
            device_id={"tool": d},
            device_id_type=MESH,
        )

    def row_copy(src, dst, ssem, rsem):
        def make(d, s):
            return pltpu.make_async_remote_copy(
                src_ref=src.at[d],
                dst_ref=dst.at[s],
                send_sem=ssem.at[d],
                recv_sem=rsem.at[s],
                device_id={"tool": d},
                device_id_type=MESH,
            )

        return make

    msg1_copy = row_copy(msg1s, msg1r, m1ss, m1rs)
    msg2_copy = row_copy(msg2s, msg2r, m2ss, m2rs)
    back_copy = [
        row_copy(backs.at[k], backr.at[k], bss.at[k], brs.at[k]) for k in range(STEPS)
    ]

    def send_all(make, first, last):
        @pl.loop(first, last)
        def _(off):
            make(partner(off), t).start()

    def wait_arrivals(make):
        @pl.loop(1, n_tool)
        def _(off):
            make(partner(off), source_of(off)).wait_recv()

    def wait_sends(make):
        @pl.loop(1, n_tool)
        def _(off):
            make(partner(off), t).wait_send()

    left = {"tool": jnp.where(has_left, t - 1, t + 1)}
    right = {"tool": jnp.where(has_right, t + 1, t - 1)}
    down = {"blank": jnp.where(has_down, b - 1, b + 1)}
    up = {"blank": jnp.where(has_up, b + 1, b - 1)}

    def x_copy(way, par, c):
        rows = pl.ds(pl.multiple_of(TILE + c * CY, TILE), CY)
        src, dst = (1, SX + 1) if way == 0 else (SX, 0)
        return pltpu.make_async_remote_copy(
            src_ref=F[par].at[src, :, rows, :],
            dst_ref=F[par].at[dst, :, rows, :],
            send_sem=xss.at[par, way, c],
            recv_sem=xrs.at[par, way, c],
            device_id=left if way == 0 else right,
            device_id_type=MESH,
        )

    def y_copy(way, par):
        return pltpu.make_async_remote_copy(
            src_ref=ys.at[par, way],
            dst_ref=yr.at[par, 1 - way],
            send_sem=yss.at[par, way],
            recv_sem=yrs.at[par, way],
            device_id=down if way == 0 else up,
            device_id_type=MESH,
        )

    def kx_copy(way):
        rows = pl.ds(TILE, SY)
        src, dst = (1, SX + 1) if way == 0 else (SX, 0)
        return pltpu.make_async_remote_copy(
            src_ref=K.at[src, :, rows, :],
            dst_ref=K.at[dst, :, rows, :],
            send_sem=kss.at[0, way],
            recv_sem=krs.at[0, way],
            device_id=left if way == 0 else right,
            device_id_type=MESH,
        )

    def ky_copy(way):
        return pltpu.make_async_remote_copy(
            src_ref=kys.at[way],
            dst_ref=kyr.at[1 - way],
            send_sem=kss.at[1, way],
            recv_sem=krs.at[1, way],
            device_id=down if way == 0 else up,
            device_id_type=MESH,
        )

    sends_x, sends_y = (has_left, has_right), (has_down, has_up)
    gets_x, gets_y = (has_right, has_left), (has_up, has_down)

    def at_each(flags, act):
        for way in range(2):
            @pl.when(flags[way])
            def _(way=way):
                act(way)

    for zb in range(ZB):
        loads[zb].wait()

    @pl.loop(0, SX)
    def _(xl):
        @pl.loop(0, ZB)
        def _(zb):
            m = mat[xl, zb]
            low, mid, top = (m & 1) != 0, (m & 2) != 0, (m & 4) != 0
            pairs = [jnp.where(low, cond[2 * i + 1], cond[2 * i]) for i in range(4)]
            quads = [jnp.where(mid, pairs[2 * i + 1], pairs[2 * i]) for i in range(2)]
            K[1 + xl, zb, pl.ds(TILE, SY), :] = jnp.where(top, quads[1], quads[0])

    at_each(sends_x, lambda way: kx_copy(way).start())

    @pl.loop(0, ZB)
    def _(zb):
        for xl in range(SX):
            kys[0, zb, pl.ds(xl, 1), :] = K[1 + xl, zb, pl.ds(TILE, 1), :]
            kys[1, zb, pl.ds(xl, 1), :] = K[1 + xl, zb, pl.ds(TILE + SY - 1, 1), :]

    at_each(sends_y, lambda way: ky_copy(way).start())

    outflow = film[...] * (theta0[...] - contact[...])
    hi, lo = split_pair(outflow)
    XB[:, 0:LANES] = hi
    XB[:, LANES : 2 * LANES] = lo
    part_rows = min(512, slots)
    step_rows = min(512, voxel_blocks)

    def pack(write, columns):
        @pl.loop(0, slots // part_rows)
        def _(i):
            got = jnp.dot(
                PM[pl.ds(pl.multiple_of(i * part_rows, part_rows), part_rows), :],
                XB[:, columns : columns + 2 * LANES],
                preferred_element_type=jnp.float32,
            )
            rows = got[:, :LANES] + got[:, LANES:]
            write(i * (part_rows // CAP), rows.reshape(part_rows // CAP, CAP, LANES))

    def write1(d, rows):
        msg1s[pl.ds(d, part_rows // CAP)] = rows

    pack(write1, 0)
    send_all(meta_copy, 1, n_tool)
    send_all(msg1_copy, 1, n_tool)
    metar[t] = metas[t // 2]
    msg1r[t] = msg1s[t]

    def pack_y(par, way):
        row = TILE if way == 0 else TILE + SY - 1

        @pl.loop(0, ZB)
        def _(zb):
            for xl in range(SX):
                ys[par, way, zb, pl.ds(xl, 1), :] = F[par][1 + xl, zb, pl.ds(row, 1), :]

    def unpack_y(par, side):
        row = TILE - 1 if side == 0 else TILE + SY

        @pl.loop(0, ZB)
        def _(zb):
            for xl in range(SX):
                F[par][1 + xl, zb, pl.ds(row, 1), :] = yr[par, side, zb, pl.ds(xl, 1), :]

    for zb in range(ZB):
        loads[ZB + zb].wait()

    @pl.loop(0, NC)
    def _(c):
        at_each(sends_x, lambda way: x_copy(way, 0, c).start())

    for way in range(2):
        pack_y(0, way)
    at_each(sends_y, lambda way: y_copy(way, 0).start())

    for j in range(BEADROWS // TILE):
        @pl.loop(0, TILE)
        def _(i, j=j):
            at = pl.ds(pl.multiple_of(i * LANES, LANES), LANES)
            shell = bead_rows[pl.ds(j * TILE + i, 1), :]
            row, lane = shell // LANES, shell % LANES
            A[:, at] = one_hot(
                lax.broadcasted_iota(jnp.int32, (BLK, LANES), 0) == jnp.broadcast_to(row, (BLK, LANES))
            )
            here = lax.broadcasted_iota(jnp.int32, (LANES, LANES), 0) == jnp.broadcast_to(lane, (LANES, LANES))
            held = jnp.where(here, jnp.broadcast_to(gain_rows[pl.ds(j * TILE + i, 1), :], (LANES, LANES)), 0.0)
            hi, lo = split_pair(held)
            BT[0:LANES, at] = hi
            BT[LANES : 2 * LANES, at] = lo

        part = lax.dot_general(
            A[...], BT[...], (((1,), (1,)), ((), ())), preferred_element_type=jnp.float32
        )
        if j == 0:
            acc[...] = part
        else:
            acc[...] += part

    sigma = 1.0 - 0.4 * jnp.tanh(theta0[...])
    rate = base_rate[...] + sigma * (acc[:, :LANES] + acc[:, LANES:])
    after = theta0[...] + shell_step * (sigma * rate - outflow)
    theta1[...] = after
    hi, lo = split_pair(film[...])
    XB[:, 0:LANES] = hi
    XB[:, LANES : 2 * LANES] = lo
    hi, lo = split_pair(film[...] * after)
    XB[:, 2 * LANES : 3 * LANES] = hi
    XB[:, 3 * LANES : 4 * LANES] = lo

    def write2(d, rows, first):
        msg2s[pl.ds(d, part_rows // CAP), first : first + CAP, :] = rows

    pack(lambda d, rows: write2(d, rows, 0), 0)
    pack(lambda d, rows: write2(d, rows, CAP), 2 * LANES)
    msg2r[t] = msg2s[t]

    lane = lax.broadcasted_iota(jnp.int32, (SY, LANES), 1)
    last_lane, first_lane = lane == LANES - 1, lane == 0

    @pl.loop(0, SX)
    def _(xl):
        line = [K[1 + xl, zb, pl.ds(TILE, SY), :] for zb in range(ZB)]
        ahead = [pltpu.roll(k, LANES - 1, 1) for k in line] + [jnp.zeros((SY, LANES), jnp.float32)]
        behind = [jnp.zeros((SY, LANES), jnp.float32)] + [pltpu.roll(k, 1, 1) for k in line]
        for zb in range(ZB):
            high = jnp.where(last_lane, ahead[zb + 1], ahead[zb])
            low = jnp.where(first_lane, behind[zb], behind[zb + 1])
            GzH[xl, zb] = face_step * (line[zb] + high)
            GzL[xl, zb] = face_step * (line[zb] + low)

    def x_faces(p):
        @pl.loop(0, ZB)
        def _(zb):
            Gx[p, zb] = face_step * (K[p, zb, pl.ds(TILE, SY), :] + K[p + 1, zb, pl.ds(TILE, SY), :])

    @pl.loop(1, SX)
    def _(p):
        x_faces(p)

    wait_arrivals(meta_copy)
    even = lax.rem(t, 2) == 0
    lin_rows = []
    for q in range(qgroups):
        first, second = metar[2 * q], metar[2 * q + 1]
        first = jnp.where(even, first, pltpu.roll(first, CAP, 1))
        second = jnp.where(even, pltpu.roll(second, CAP, 1), second)
        lin = jnp.where(lane8 < CAP, first, second)
        lin_rows.append(lin)
        gidx_v[pl.ds(q, 1), :] = jnp.maximum(lin[0:1], 0)
    to_smem = pltpu.make_async_copy(gidx_v, gidx_s, idx_sem)
    to_smem.start()

    @pl.loop(0, voxel_blocks // LANES)
    def _(i):
        rows = lax.broadcasted_iota(jnp.int32, (LANES, LANES), 0) + i * LANES
        for q in range(qgroups):
            O[pl.ds(pl.multiple_of(i * LANES, LANES), LANES), q * LANES : (q + 1) * LANES] = one_hot(
                rows == jnp.broadcast_to(lin_rows[q][0:1], (LANES, LANES))
            )

    to_smem.wait()

    at_each(gets_y, lambda way: ky_copy(way).wait_recv())

    @pl.loop(0, ZB)
    def _(zb):
        for xl in range(SX):
            K[1 + xl, zb, pl.ds(TILE - 1, 1), :] = kyr[0, zb, pl.ds(xl, 1), :]
            K[1 + xl, zb, pl.ds(TILE + SY, 1), :] = kyr[1, zb, pl.ds(xl, 1), :]

    @pl.loop(0, SX)
    def _(xl):
        @pl.loop(0, ZB)
        def _(zb):
            Gy[xl, zb, pl.ds(TILE - 1, 1), :] = face_step * (
                K[1 + xl, zb, pl.ds(TILE - 1, 1), :] + K[1 + xl, zb, pl.ds(TILE, 1), :]
            )
            Gy[xl, zb, pl.ds(TILE, SY), :] = face_step * (
                K[1 + xl, zb, pl.ds(TILE, SY), :] + K[1 + xl, zb, pl.ds(TILE + 1, SY), :]
            )

    at_each(gets_x, lambda way: kx_copy(way).wait_recv())
    x_faces(0)
    x_faces(SX)

    def split_rows(src, rows, first, column):
        @pl.loop(0, n_tool)
        def _(s):
            hi, lo = split_pair(src[s, first : first + rows, :])
            at = pl.ds(pl.multiple_of(s * CAP, CAP), CAP)
            R[at, column : column + LANES] = hi
            R[at, column + LANES : column + 2 * LANES] = lo

    def scatter(column, write):
        @pl.loop(0, voxel_blocks // step_rows)
        def _(m):
            at = pl.ds(pl.multiple_of(m * step_rows, step_rows), step_rows)
            got = jnp.dot(
                O[at, :], R[:, column : column + 2 * LANES], preferred_element_type=jnp.float32
            )
            write(at, source_step * (got[:, :LANES] + got[:, LANES:]))

    def to_source(at, rows):
        SRC[at, :] = rows

    def to_weight(at, rows):
        W[at, :] = rows

    wait_arrivals(msg1_copy)
    split_rows(msg1r, CAP, 0, 0)
    scatter(0, to_source)

    lane_t = lax.broadcasted_iota(jnp.int32, (TILE, LANES), 1)
    top_lane, low_lane = lane_t == LANES - 1, lane_t == 0
    no_heat = jnp.zeros((TILE, LANES), jnp.float32)

    def planes(par, y0, first, last):
        old, new = F[par], F[1 - par]
        y0 = pl.multiple_of(y0, TILE)
        rows = pl.ds(pl.multiple_of(y0 + TILE, TILE), TILE)
        all_z = range(ZB)

        def temp(p, zb, shift=0):
            return old[p, zb, rows if shift == 0 else pl.ds(y0 + TILE + shift, TILE), :]

        center = [temp(first, zb) for zb in all_z]
        below = [Gx[first - 1, zb, pl.ds(y0, TILE), :] * (center[zb] - temp(first - 1, zb)) for zb in all_z]
        for p in range(first, last):
            xl = p - 1
            ahead = [temp(p + 1, zb) for zb in all_z]
            above = [Gx[p, zb, pl.ds(y0, TILE), :] * (ahead[zb] - center[zb]) for zb in all_z]
            after = [pltpu.roll(now, LANES - 1, 1) for now in center] + [no_heat]
            before = [no_heat] + [pltpu.roll(now, 1, 1) for now in center]
            for zb in all_z:
                now = center[zb]
                z_high = GzH[xl, zb, pl.ds(y0, TILE), :] * (jnp.where(top_lane, after[zb + 1], after[zb]) - now)
                z_low = GzL[xl, zb, pl.ds(y0, TILE), :] * (now - jnp.where(low_lane, before[zb], before[zb + 1]))
                y_high = Gy[xl, zb, rows, :] * (temp(p, zb, 1) - now)
                y_low = Gy[xl, zb, pl.ds(y0 + TILE - 1, TILE), :] * (now - temp(p, zb, -1))
                at = pl.multiple_of((xl * ZB + zb) * SY + y0, TILE)
                total = (above[zb] - below[zb]) + (y_high - y_low) + (z_high - z_low)
                new[p, zb, rows, :] = now + (total + SRC[pl.ds(at, TILE), :])
            center, below = ahead, above

    def keep(cur, with_source):
        @pl.loop(0, SX)
        def _(xl):
            @pl.loop(0, ZB)
            def _(zb):
                at = pl.ds(pl.multiple_of((xl * ZB + zb) * SY, SY), SY)
                now = F[cur][1 + xl, zb, pl.ds(TILE, SY), :]
                FG[at, :] = now
                if with_source:
                    SRC[at, :] = SRC[at, :] - W[at, :] * now

    def collect(k):
        @pl.loop(0, n_tool)
        def _(s):
            q = s // 2
            lane0 = lax.rem(s, 2) * CAP

            @pl.loop(0, CAP // TILE)
            def _(j):
                for i in range(TILE):
                    row = gidx_s[q, lane0 + j * TILE + i]
                    backs[k, s, pl.ds(pl.multiple_of(j * TILE, TILE) + i, 1), :] = FG[pl.ds(row, 1), :]

    total_sweeps = STEPS * SWEEPS

    def sweep(s, par):
        new = 1 - par
        more = s < total_sweeps - 1

        @pl.loop(0, NC)
        def _(k):
            c = jnp.where(k == 0, 0, jnp.where(k == 1, NC - 1, k - 1))
            first, last = k == 0, k == 1

            @pl.when(first)
            def _():
                @pl.when(has_down)
                def _():
                    y_copy(1, par).wait_recv()

                unpack_y(par, 0)

            @pl.when(last)
            def _():
                @pl.when(has_up)
                def _():
                    y_copy(0, par).wait_recv()

                unpack_y(par, 1)

            at_each(gets_x, lambda way: x_copy(way, par, c).wait_recv())

            @pl.when(s >= 1)
            def _():
                at_each(sends_x, lambda way: x_copy(way, new, c).wait_send())

            @pl.loop(0, CY // TILE)
            def _(i):
                planes(par, c * CY + i * TILE, 1, 2)
                planes(par, c * CY + i * TILE, SX, SX + 1)

            @pl.when(more)
            def _():
                at_each(sends_x, lambda way: x_copy(way, new, c).start())

            @pl.loop(0, CY // TILE)
            def _(i):
                planes(par, c * CY + i * TILE, 2, SX)

            def send_y(way):
                @pl.when(s >= 1)
                def _():
                    y_copy(way, new).wait_send()

                @pl.when(more)
                def _():
                    pack_y(new, way)
                    y_copy(way, new).start()

            @pl.when(first & has_down)
            def _():
                send_y(0)

            @pl.when(last & has_up)
            def _():
                send_y(1)

    @pl.loop(0, total_sweeps // 2)
    def _(pair):
        sweep(2 * pair, 0)
        half = (n_tool + 1) // 2

        @pl.when(pair == 0)
        def _():
            send_all(msg2_copy, 1, half)

        @pl.when(pair == 1)
        def _():
            wait_arrivals(msg2_copy)
            split_rows(msg2r, CAP, 0, 0)
            split_rows(msg2r, CAP, CAP, 2 * LANES)
            scatter(0, to_weight)

        @pl.when(pair == 2)
        def _():
            collect(0)
            send_all(back_copy[0], 1, half)

        sweep(2 * pair + 1, 1)

        @pl.when(pair == 0)
        def _():
            send_all(msg2_copy, half, n_tool)

        @pl.when(pair == 1)
        def _():
            scatter(2 * LANES, to_source)
            keep(0, True)

        @pl.when(pair == 2)
        def _():
            send_all(back_copy[0], half, n_tool)

    keep(0, False)
    stores = [
        pltpu.make_async_copy(
            FG.at[pl.ds((xl * ZB + zb) * SY, SY), :],
            tool_out.at[xl, :, pl.ds(zb * LANES, LANES)],
            out_sem.at[xl, zb],
        )
        for xl in range(SX)
        for zb in range(ZB)
    ]
    collect(1)
    send_all(back_copy[1], 1, n_tool)
    for copy in stores:
        copy.start()

    def contact_of(k):
        backr[k, t] = backs[k, t]
        wait_arrivals(back_copy[k])
        split_rows(backr.at[k], CAP, 0, 0)
        got = jnp.dot(PT[...], R[:, 0 : 2 * LANES], preferred_element_type=jnp.float32)
        return got[:, :LANES] + got[:, LANES:]

    flux = film[...] * (contact_of(0) - theta1[...])
    sigma = 1.0 - 0.4 * jnp.tanh(theta1[...])
    rate = base_rate[...] + sigma * (acc[:, :LANES] + acc[:, LANES:])
    shell_out[...] = theta1[...] + shell_step * (flux + sigma * rate)
    contact_out[...] = contact_of(1)

    wait_sends(meta_copy)
    wait_sends(msg1_copy)
    wait_sends(msg2_copy)
    wait_sends(back_copy[0])
    wait_sends(back_copy[1])
    at_each(sends_x, lambda way: kx_copy(way).wait_send())
    at_each(sends_y, lambda way: ky_copy(way).wait_send())

    @pl.loop(0, NC)
    def _(c):
        at_each(sends_x, lambda way: x_copy(way, 1, c).wait_send())

    at_each(sends_y, lambda way: y_copy(way, 1).wait_send())

    for copy in stores:
        copy.wait()


MESH = pl.DeviceIdType.MESH


def on_device(n_tool, n_blank, tool_temp, material, conductivity, shell_temp, base_rate, film, contact_temp, pair_slab, pair_block, bead_ids, bead_gain):
    SX, SY, SZ = tool_temp.shape
    ZB = SZ // LANES
    NC = CHUNKS
    BLK = shell_temp.shape[0]
    beadrows = bead_ids.shape[0] // LANES
    slots = n_tool * CAP
    voxel_blocks = SX * SY * ZB
    f32, bf16, i32 = jnp.float32, jnp.bfloat16, jnp.int32
    V = pltpu.VMEM
    dma = pltpu.SemaphoreType.DMA
    scratch = [
        V((SX + 2, ZB, SY + 2 * TILE, LANES), f32),
        V((SX + 2, ZB, SY + 2 * TILE, LANES), f32),
        V((SX + 2, ZB, SY + 2 * TILE, LANES), f32),
        V((SX, ZB, SY, LANES), i32),
        V((SX + 1, ZB, SY, LANES), f32),
        V((SX, ZB, SY + TILE, LANES), f32),
        V((SX, ZB, SY, LANES), f32),
        V((SX, ZB, SY, LANES), f32),
        V((voxel_blocks, LANES), f32),
        V((voxel_blocks, LANES), f32),
        V((voxel_blocks, LANES), f32),
        V((voxel_blocks, slots), bf16),
        V((slots, BLK), bf16),
        V((BLK, slots), bf16),
        V((BLK, 4 * LANES), bf16),
        V((slots, 4 * LANES), bf16),
        V((BLK, TILE * LANES), bf16),
        V((2 * LANES, TILE * LANES), bf16),
        V((BLK, 2 * LANES), f32),
        V((BLK, LANES), i32),
        V((BLK, LANES), i32),
        V((slots // LANES, TILE, LANES), i32),
        V((n_tool, TILE, LANES), i32),
        V((slots // LANES, LANES), i32),
        pltpu.SMEM((slots // LANES, LANES), i32),
        V((2, 2, ZB, SX, LANES), f32),
        V((2, 2, ZB, SX, LANES), f32),
        V((2, ZB, SX, LANES), f32),
        V((2, ZB, SX, LANES), f32),
        V((n_tool, CAP, LANES), f32),
        V((n_tool, CAP, LANES), f32),
        V((n_tool, 2 * CAP, LANES), f32),
        V((n_tool, 2 * CAP, LANES), f32),
        V((STEPS, n_tool, CAP, LANES), f32),
        V((STEPS, n_tool, CAP, LANES), f32),
        V((BLK, LANES), f32),
        dma((2, ZB)),
        dma((SX, ZB)),
        dma,
        dma((2, 2, NC)),
        dma((2, 2, NC)),
        dma((2, 2)),
        dma((2, 2)),
        dma((2, 2)),
        dma((2, 2)),
        dma((n_tool,)),
        dma((n_tool,)),
        dma((n_tool,)),
        dma((n_tool,)),
        dma((n_tool,)),
        dma((n_tool,)),
        dma((STEPS, n_tool)),
        dma((STEPS, n_tool)),
    ]
    whole = pl.BlockSpec(memory_space=pltpu.VMEM)
    far = pl.BlockSpec(memory_space=pl.ANY)
    return pl.pallas_call(
        functools.partial(kernel, (n_tool, n_blank, SX, SY, ZB, BLK, beadrows)),
        out_shape=(
            jax.ShapeDtypeStruct(tool_temp.shape, f32),
            jax.ShapeDtypeStruct(shell_temp.shape, f32),
            jax.ShapeDtypeStruct(shell_temp.shape, f32),
        ),
        in_specs=[far, far, pl.BlockSpec(memory_space=pltpu.SMEM)] + [whole] * 8,
        out_specs=(far, whole, whole),
        scratch_shapes=scratch,
        compiler_params=pltpu.CompilerParams(
            collective_id=0, has_side_effects=True, vmem_limit_bytes=60 * 2**20
        ),
    )(
        tool_temp,
        material,
        conductivity,
        shell_temp,
        base_rate,
        film,
        contact_temp,
        pair_slab.reshape(BLK // LANES, LANES),
        pair_block.reshape(BLK // LANES, LANES),
        bead_ids.reshape(beadrows, LANES),
        bead_gain.reshape(beadrows, LANES),
    )


def solution(mesh):
    placed = (
        P("tool", "blank", None),
        P("tool", "blank", None),
        P(),
        P(("blank", "tool"), None),
        P(("blank", "tool"), None),
        P(("blank", "tool"), None),
        P(("blank", "tool"), None),
        P(("blank", "tool"), None),
        P(("blank", "tool")),
        P(("blank", "tool")),
        P(("blank", "tool")),
    )
    return jax.shard_map(
        functools.partial(on_device, mesh.shape["tool"], mesh.shape["blank"]),
        mesh=mesh,
        in_specs=placed,
        out_specs=(
            P("tool", "blank", None),
            P(("blank", "tool"), None),
            P(("blank", "tool"), None),
        ),
        check_vma=False,
    )
```

```python
import functools
import math

import jax
import jax.numpy as jnp
from jax import lax
from jax.experimental import pallas as pl
from jax.experimental.pallas import tpu as pltpu
from jax.sharding import PartitionSpec as P

STEPS = 2
SWEEPS = 4
CAP = 64
LANES = 128
TILE = 8
CHUNKS = 4

diffuse_step = 0.12
source_step = 0.25
shell_step = 0.5
face_step = 0.5 * diffuse_step


def split_pair(x):
    hi = x.astype(jnp.bfloat16)
    lo = (x - hi.astype(jnp.float32)).astype(jnp.bfloat16)
    return hi, lo


def one_hot(mask):
    return jnp.where(mask, 1.0, 0.0).astype(jnp.bfloat16)


def fold_rows(acc):
    for shift in (4, 2, 1):
        acc = acc + pltpu.roll(acc, shift, 0)
    return acc


def column_of(row):
    return jnp.transpose(jnp.broadcast_to(row, (LANES, LANES)))


def kernel(
    dims,
    tool_hbm,
    mat_hbm,
    cond,
    theta0,
    base_rate,
    film,
    contact,
    slab_rows,
    block_rows,
    bead_rows,
    gain_rows,
    tool_out,
    shell_out,
    contact_out,
    FA,
    FB,
    K,
    mat,
    Gx,
    Gy,
    GzH,
    GzL,
    SRC,
    W,
    BD,
    FG,
    O,
    PM,
    PT,
    XB,
    R,
    A,
    BT,
    acc,
    slot_col,
    lin_col,
    metas,
    metar,
    gidx_v,
    gidx_s,
    ys,
    yr,
    kys,
    kyr,
    msg1s,
    msg1r,
    msgWs,
    msgWr,
    msgBs,
    msgBr,
    backs,
    backr,
    theta1,
    load_sem,
    out_sem,
    idx_sem,
    xss,
    xrs,
    yss,
    yrs,
    kss,
    krs,
    metass,
    metars,
    m1ss,
    m1rs,
    mWss,
    mWrs,
    mBss,
    mBrs,
    bss,
    brs,
):
    n_tool, n_blank, SX, SY, ZB, BLK, BEADROWS = dims
    slots = n_tool * CAP
    voxel_blocks = SX * SY * ZB
    NC = CHUNKS
    CY = SY // NC
    F = (FA, FB)
    groups = BLK // LANES
    qgroups = slots // LANES
    t = lax.axis_index("tool")
    b = lax.axis_index("blank")
    has_left, has_right = t > 0, t < n_tool - 1
    has_down, has_up = b > 0, b < n_blank - 1

    loads = []
    for zb in range(ZB):
        loads.append(
            pltpu.make_async_copy(
                mat_hbm.at[:, :, pl.ds(zb * LANES, LANES)],
                mat.at[:, zb],
                load_sem.at[1, zb],
            )
        )
    for zb in range(ZB):
        loads.append(
            pltpu.make_async_copy(
                tool_hbm.at[:, :, pl.ds(zb * LANES, LANES)],
                FA.at[pl.ds(1, SX), zb, pl.ds(TILE, SY), :],
                load_sem.at[0, zb],
            )
        )
    for copy in loads:
        copy.start()

    barrier = pltpu.get_barrier_semaphore()

    @pl.loop(1, n_tool)
    def _(off):
        pl.semaphore_signal(
            barrier, inc=1, device_id={"tool": lax.rem(t + off, n_tool)}, device_id_type=MESH
        )

    @pl.when(has_down)
    def _():
        pl.semaphore_signal(barrier, inc=1, device_id={"blank": b - 1}, device_id_type=MESH)

    @pl.when(has_up)
    def _():
        pl.semaphore_signal(barrier, inc=1, device_id={"blank": b + 1}, device_id_type=MESH)

    def clear_plane(plane):
        @pl.loop(0, ZB)
        def _(zb):
            zeros = jnp.zeros((SY, LANES), jnp.float32)
            K[plane, zb, pl.ds(TILE, SY), :] = zeros
            FA[plane, zb, pl.ds(TILE, SY), :] = zeros
            FB[plane, zb, pl.ds(TILE, SY), :] = zeros

    @pl.when(jnp.logical_not(has_left))
    def _():
        clear_plane(0)

    @pl.when(jnp.logical_not(has_right))
    def _():
        clear_plane(SX + 1)

    def clear_rim(side):
        zeros = jnp.zeros((ZB, SX, LANES), jnp.float32)
        yr[0, side] = zeros
        yr[1, side] = zeros
        kyr[side] = zeros

    @pl.when(jnp.logical_not(has_down))
    def _():
        clear_rim(0)

    @pl.when(jnp.logical_not(has_up))
    def _():
        clear_rim(1)

    sub8 = lax.broadcasted_iota(jnp.int32, (TILE, LANES), 0)
    lane8 = lax.broadcasted_iota(jnp.int32, (TILE, LANES), 1)

    def row8(ref, g):
        return jnp.broadcast_to(ref[pl.ds(g, 1), :], (TILE, LANES))

    for g in range(groups):
        slot_col[pl.ds(g * LANES, LANES), :] = column_of(slab_rows[pl.ds(g, 1), :])
        blk = block_rows[pl.ds(g, 1), :]
        yl = (blk // ZB) % SY
        lin = ((blk // (ZB * SY)) * ZB + blk % ZB) * SY + yl
        lin_col[pl.ds(g * LANES, LANES), :] = column_of(lin)

    slot_rows = []
    for g in range(groups):
        mine = row8(slab_rows, g)

        def count(i, total, mine=mine, g=g):
            other = slot_col[pl.ds(pl.multiple_of(i * TILE, TILE), TILE), :]
            before = (sub8 + i * TILE) < (lane8 + g * LANES)
            return total + jnp.where((other == mine) & before, 1, 0)

        rank = fold_rows(
            lax.fori_loop(0, (g + 1) * LANES // TILE, count, jnp.zeros((TILE, LANES), jnp.int32))
        )
        slot_rows.append(mine * CAP + rank)
    for g in range(groups):
        slot_col[pl.ds(g * LANES, LANES), :] = column_of(slot_rows[g][0:1])

    @pl.loop(0, slots // LANES)
    def _(i):
        rows = lax.broadcasted_iota(jnp.int32, (LANES, LANES), 0) + i * LANES
        for g in range(groups):
            PM[pl.ds(pl.multiple_of(i * LANES, LANES), LANES), g * LANES : (g + 1) * LANES] = one_hot(
                rows == jnp.broadcast_to(slot_rows[g][0:1], (LANES, LANES))
            )

    @pl.loop(0, qgroups)
    def _(q):
        def part(i, total):
            at = pl.ds(pl.multiple_of(i * 16, 16), 16)
            hit = slot_col[at, :] == (lax.broadcasted_iota(jnp.int32, (16, LANES), 1) + q * LANES)
            PT[at, pl.ds(pl.multiple_of(q * LANES, LANES), LANES)] = one_hot(hit)
            named = jnp.where(hit, lin_col[at, :] + 1, 0)
            return total + named[:TILE] + named[TILE:]

        total = lax.fori_loop(0, BLK // 16, part, jnp.zeros((TILE, LANES), jnp.int32), unroll=4)
        metas[q] = fold_rows(total) - 1

    outflow = film[...] * (theta0[...] - contact[...])
    hi, lo = split_pair(outflow)
    XB[:, 0:LANES] = hi
    XB[:, LANES : 2 * LANES] = lo
    part_rows = min(512, slots)
    step_rows = min(512, voxel_blocks)

    def pack(write, columns):
        @pl.loop(0, slots // part_rows)
        def _(i):
            got = jnp.dot(
                PM[pl.ds(pl.multiple_of(i * part_rows, part_rows), part_rows), :],
                XB[:, columns : columns + 2 * LANES],
                preferred_element_type=jnp.float32,
            )
            rows = got[:, :LANES] + got[:, LANES:]
            write(i * (part_rows // CAP), rows.reshape(part_rows // CAP, CAP, LANES))

    def write1(d, rows):
        msg1s[pl.ds(d, part_rows // CAP)] = rows

    pack(write1, 0)

    pl.semaphore_wait(barrier, n_tool - 1 + jnp.where(has_down, 1, 0) + jnp.where(has_up, 1, 0))

    side = math.isqrt(n_tool)
    row, column = t // side, lax.rem(t, side)

    def partner(k):
        step = lax.rem(k * 7, n_tool)
        return lax.rem(row + step // side, side) * side + lax.rem(column + lax.rem(step, side), side)

    def source_of(k):
        step = lax.rem(k * 7, n_tool)
        return lax.rem(row + side - step // side, side) * side + lax.rem(column + side - lax.rem(step, side), side)

    def meta_copy(d, s):
        return pltpu.make_async_remote_copy(
            src_ref=metas.at[d // 2],
            dst_ref=metar.at[s],
            send_sem=metass.at[d],
            recv_sem=metars.at[s],
            device_id={"tool": d},
            device_id_type=MESH,
        )

    def row_copy(src, dst, ssem, rsem):
        def make(d, s):
            return pltpu.make_async_remote_copy(
                src_ref=src.at[d],
                dst_ref=dst.at[s],
                send_sem=ssem.at[d],
                recv_sem=rsem.at[s],
                device_id={"tool": d},
                device_id_type=MESH,
            )

        return make

    msg1_copy = row_copy(msg1s, msg1r, m1ss, m1rs)
    msgW_copy = row_copy(msgWs, msgWr, mWss, mWrs)
    msgB_copy = row_copy(msgBs, msgBr, mBss, mBrs)
    back_copy = [
        row_copy(backs.at[k], backr.at[k], bss.at[k], brs.at[k]) for k in range(STEPS)
    ]

    def send_all(make, first, last):
        @pl.loop(first, last)
        def _(off):
            make(partner(off), t).start()

    def wait_arrivals(make):
        @pl.loop(1, n_tool)
        def _(off):
            make(partner(off), source_of(off)).wait_recv()

    def wait_sends(make):
        @pl.loop(1, n_tool)
        def _(off):
            make(partner(off), t).wait_send()

    left = {"tool": jnp.where(has_left, t - 1, t + 1)}
    right = {"tool": jnp.where(has_right, t + 1, t - 1)}
    down = {"blank": jnp.where(has_down, b - 1, b + 1)}
    up = {"blank": jnp.where(has_up, b + 1, b - 1)}

    def x_copy(way, par, c):
        rows = pl.ds(pl.multiple_of(TILE + c * CY, TILE), CY)
        src, dst = (1, SX + 1) if way == 0 else (SX, 0)
        return pltpu.make_async_remote_copy(
            src_ref=F[par].at[src, :, rows, :],
            dst_ref=F[par].at[dst, :, rows, :],
            send_sem=xss.at[par, way, c],
            recv_sem=xrs.at[par, way, c],
            device_id=left if way == 0 else right,
            device_id_type=MESH,
        )

    def y_copy(way, par):
        return pltpu.make_async_remote_copy(
            src_ref=ys.at[par, way],
            dst_ref=yr.at[par, 1 - way],
            send_sem=yss.at[par, way],
            recv_sem=yrs.at[par, way],
            device_id=down if way == 0 else up,
            device_id_type=MESH,
        )

    def kx_copy(way):
        rows = pl.ds(TILE, SY)
        src, dst = (1, SX + 1) if way == 0 else (SX, 0)
        return pltpu.make_async_remote_copy(
            src_ref=K.at[src, :, rows, :],
            dst_ref=K.at[dst, :, rows, :],
            send_sem=kss.at[0, way],
            recv_sem=krs.at[0, way],
            device_id=left if way == 0 else right,
            device_id_type=MESH,
        )

    def ky_copy(way):
        return pltpu.make_async_remote_copy(
            src_ref=kys.at[way],
            dst_ref=kyr.at[1 - way],
            send_sem=kss.at[1, way],
            recv_sem=krs.at[1, way],
            device_id=down if way == 0 else up,
            device_id_type=MESH,
        )

    sends_x, sends_y = (has_left, has_right), (has_down, has_up)
    gets_x, gets_y = (has_right, has_left), (has_up, has_down)

    def at_each(flags, act):
        for way in range(2):
            @pl.when(flags[way])
            def _(way=way):
                act(way)

    send_all(meta_copy, 1, n_tool)
    send_all(msg1_copy, 1, n_tool)
    metar[t] = metas[t // 2]
    msg1r[t] = msg1s[t]

    for zb in range(ZB):
        loads[zb].wait()

    @pl.loop(0, SX)
    def _(xl):
        @pl.loop(0, ZB)
        def _(zb):
            m = mat[xl, zb]
            low, mid, top = (m & 1) != 0, (m & 2) != 0, (m & 4) != 0
            pairs = [jnp.where(low, cond[2 * i + 1], cond[2 * i]) for i in range(4)]
            quads = [jnp.where(mid, pairs[2 * i + 1], pairs[2 * i]) for i in range(2)]
            K[1 + xl, zb, pl.ds(TILE, SY), :] = jnp.where(top, quads[1], quads[0])

    at_each(sends_x, lambda way: kx_copy(way).start())

    @pl.loop(0, ZB)
    def _(zb):
        for xl in range(SX):
            kys[0, zb, pl.ds(xl, 1), :] = K[1 + xl, zb, pl.ds(TILE, 1), :]
            kys[1, zb, pl.ds(xl, 1), :] = K[1 + xl, zb, pl.ds(TILE + SY - 1, 1), :]

    at_each(sends_y, lambda way: ky_copy(way).start())

    def pack_y(par, way):
        row = TILE if way == 0 else TILE + SY - 1

        @pl.loop(0, ZB)
        def _(zb):
            for xl in range(SX):
                ys[par, way, zb, pl.ds(xl, 1), :] = F[par][1 + xl, zb, pl.ds(row, 1), :]

    def unpack_y(par, side):
        row = TILE - 1 if side == 0 else TILE + SY

        @pl.loop(0, ZB)
        def _(zb):
            for xl in range(SX):
                F[par][1 + xl, zb, pl.ds(row, 1), :] = yr[par, side, zb, pl.ds(xl, 1), :]

    for zb in range(ZB):
        loads[ZB + zb].wait()

    for way in range(2):
        pack_y(0, way)
    at_each(sends_y, lambda way: y_copy(way, 0).start())

    for j in range(BEADROWS // TILE):
        @pl.loop(0, TILE)
        def _(i, j=j):
            at = pl.ds(pl.multiple_of(i * LANES, LANES), LANES)
            shell = bead_rows[pl.ds(j * TILE + i, 1), :]
            row, lane = shell // LANES, shell % LANES
            A[:, at] = one_hot(
                lax.broadcasted_iota(jnp.int32, (BLK, LANES), 0) == jnp.broadcast_to(row, (BLK, LANES))
            )
            here = lax.broadcasted_iota(jnp.int32, (LANES, LANES), 0) == jnp.broadcast_to(lane, (LANES, LANES))
            held = jnp.where(here, jnp.broadcast_to(gain_rows[pl.ds(j * TILE + i, 1), :], (LANES, LANES)), 0.0)
            hi, lo = split_pair(held)
            BT[0:LANES, at] = hi
            BT[LANES : 2 * LANES, at] = lo

        part = lax.dot_general(
            A[...], BT[...], (((1,), (1,)), ((), ())), preferred_element_type=jnp.float32
        )
        if j == 0:
            acc[...] = part
        else:
            acc[...] += part

    sigma = 1.0 - 0.4 * jnp.tanh(theta0[...])
    rate = base_rate[...] + sigma * (acc[:, :LANES] + acc[:, LANES:])
    after = theta0[...] + shell_step * (sigma * rate - outflow)
    theta1[...] = after
    hi, lo = split_pair(film[...])
    XB[:, 0:LANES] = hi
    XB[:, LANES : 2 * LANES] = lo
    hi, lo = split_pair(film[...] * after)
    XB[:, 2 * LANES : 3 * LANES] = hi
    XB[:, 3 * LANES : 4 * LANES] = lo

    def writeW(d, rows):
        msgWs[pl.ds(d, part_rows // CAP)] = rows

    def writeB(d, rows):
        msgBs[pl.ds(d, part_rows // CAP)] = rows

    pack(writeW, 0)
    pack(writeB, 2 * LANES)
    msgWr[t] = msgWs[t]
    msgBr[t] = msgBs[t]

    @pl.loop(0, NC)
    def _(c):
        at_each(sends_x, lambda way: x_copy(way, 0, c).start())

    lane = lax.broadcasted_iota(jnp.int32, (SY, LANES), 1)
    last_lane, first_lane = lane == LANES - 1, lane == 0

    @pl.loop(0, SX)
    def _(xl):
        line = [K[1 + xl, zb, pl.ds(TILE, SY), :] for zb in range(ZB)]
        ahead = [pltpu.roll(k, LANES - 1, 1) for k in line] + [jnp.zeros((SY, LANES), jnp.float32)]
        behind = [jnp.zeros((SY, LANES), jnp.float32)] + [pltpu.roll(k, 1, 1) for k in line]
        for zb in range(ZB):
            high = jnp.where(last_lane, ahead[zb + 1], ahead[zb])
            low = jnp.where(first_lane, behind[zb], behind[zb + 1])
            GzH[xl, zb] = face_step * (line[zb] + high)
            GzL[xl, zb] = face_step * (line[zb] + low)

    def x_faces(p):
        @pl.loop(0, ZB)
        def _(zb):
            Gx[p, zb] = face_step * (K[p, zb, pl.ds(TILE, SY), :] + K[p + 1, zb, pl.ds(TILE, SY), :])

    @pl.loop(1, SX)
    def _(p):
        x_faces(p)

    wait_arrivals(meta_copy)
    even = lax.rem(t, 2) == 0
    lin_rows = []
    for q in range(qgroups):
        first, second = metar[2 * q], metar[2 * q + 1]
        first = jnp.where(even, first, pltpu.roll(first, CAP, 1))
        second = jnp.where(even, pltpu.roll(second, CAP, 1), second)
        lin = jnp.where(lane8 < CAP, first, second)
        lin_rows.append(lin)
        gidx_v[pl.ds(q, 1), :] = jnp.maximum(lin[0:1], 0)
    to_smem = pltpu.make_async_copy(gidx_v, gidx_s, idx_sem)
    to_smem.start()

    @pl.loop(0, voxel_blocks // LANES)
    def _(i):
        rows = lax.broadcasted_iota(jnp.int32, (LANES, LANES), 0) + i * LANES
        for q in range(qgroups):
            O[pl.ds(pl.multiple_of(i * LANES, LANES), LANES), q * LANES : (q + 1) * LANES] = one_hot(
                rows == jnp.broadcast_to(lin_rows[q][0:1], (LANES, LANES))
            )

    to_smem.wait()

    at_each(gets_y, lambda way: ky_copy(way).wait_recv())

    @pl.loop(0, ZB)
    def _(zb):
        for xl in range(SX):
            K[1 + xl, zb, pl.ds(TILE - 1, 1), :] = kyr[0, zb, pl.ds(xl, 1), :]
            K[1 + xl, zb, pl.ds(TILE + SY, 1), :] = kyr[1, zb, pl.ds(xl, 1), :]

    @pl.loop(0, SX)
    def _(xl):
        @pl.loop(0, ZB)
        def _(zb):
            Gy[xl, zb, pl.ds(TILE - 1, 1), :] = face_step * (
                K[1 + xl, zb, pl.ds(TILE - 1, 1), :] + K[1 + xl, zb, pl.ds(TILE, 1), :]
            )
            Gy[xl, zb, pl.ds(TILE, SY), :] = face_step * (
                K[1 + xl, zb, pl.ds(TILE, SY), :] + K[1 + xl, zb, pl.ds(TILE + 1, SY), :]
            )

    def split_rows(src):
        @pl.loop(0, n_tool)
        def _(s):
            hi, lo = split_pair(src[s])
            at = pl.ds(pl.multiple_of(s * CAP, CAP), CAP)
            R[at, 0:LANES] = hi
            R[at, LANES : 2 * LANES] = lo

    def scatter(write):
        @pl.loop(0, voxel_blocks // step_rows)
        def _(m):
            at = pl.ds(pl.multiple_of(m * step_rows, step_rows), step_rows)
            got = jnp.dot(
                O[at, :], R[...], preferred_element_type=jnp.float32
            )
            write(at, source_step * (got[:, :LANES] + got[:, LANES:]))

    def to_source(at, rows):
        SRC[at, :] = rows

    def to_weight(at, rows):
        W[at, :] = rows

    def to_rest(at, rows):
        BD[at, :] = rows

    wait_arrivals(msg1_copy)
    split_rows(msg1r)
    scatter(to_source)

    at_each(gets_x, lambda way: kx_copy(way).wait_recv())
    x_faces(0)
    x_faces(SX)

    lane_t = lax.broadcasted_iota(jnp.int32, (TILE, LANES), 1)
    top_lane, low_lane = lane_t == LANES - 1, lane_t == 0
    no_heat = jnp.zeros((TILE, LANES), jnp.float32)

    def planes(par, y0, first, last, final):
        old, new = F[par], F[1 - par]
        y0 = pl.multiple_of(y0, TILE)
        rows = pl.ds(pl.multiple_of(y0 + TILE, TILE), TILE)
        all_z = range(ZB)

        def temp(p, zb, shift=0):
            return old[p, zb, rows if shift == 0 else pl.ds(y0 + TILE + shift, TILE), :]

        center = [temp(first, zb) for zb in all_z]
        below = [Gx[first - 1, zb, pl.ds(y0, TILE), :] * (center[zb] - temp(first - 1, zb)) for zb in all_z]
        for p in range(first, last):
            xl = p - 1
            ahead = [temp(p + 1, zb) for zb in all_z]
            above = [Gx[p, zb, pl.ds(y0, TILE), :] * (ahead[zb] - center[zb]) for zb in all_z]
            after = [pltpu.roll(now, LANES - 1, 1) for now in center] + [no_heat]
            before = [no_heat] + [pltpu.roll(now, 1, 1) for now in center]
            for zb in all_z:
                now = center[zb]
                z_high = GzH[xl, zb, pl.ds(y0, TILE), :] * (jnp.where(top_lane, after[zb + 1], after[zb]) - now)
                z_low = GzL[xl, zb, pl.ds(y0, TILE), :] * (now - jnp.where(low_lane, before[zb], before[zb + 1]))
                y_high = Gy[xl, zb, rows, :] * (temp(p, zb, 1) - now)
                y_low = Gy[xl, zb, pl.ds(y0 + TILE - 1, TILE), :] * (now - temp(p, zb, -1))
                at = pl.multiple_of((xl * ZB + zb) * SY + y0, TILE)
                total = (above[zb] - below[zb]) + (y_high - y_low) + (z_high - z_low)
                result = now + (total + SRC[pl.ds(at, TILE), :])
                if final:
                    FG[pl.ds(at, TILE), :] = result
                else:
                    new[p, zb, rows, :] = result
            center, below = ahead, above

    def collect(k, d):
        q = d // 2
        lane0 = lax.rem(d, 2) * CAP

        @pl.loop(0, CAP // TILE)
        def _(j):
            for i in range(TILE):
                row = gidx_s[q, lane0 + j * TILE + i]
                backs[k, d, pl.ds(pl.multiple_of(j * TILE, TILE) + i, 1), :] = FG[pl.ds(row, 1), :]

    def collect_and_send(k):
        @pl.loop(1, n_tool)
        def _(off):
            d = partner(off)
            collect(k, d)
            back_copy[k](d, t).start()

        collect(k, t)

    def next_source(c):
        @pl.loop(0, SX)
        def _(xl):
            for zb in range(ZB):
                at = pl.ds(pl.multiple_of((xl * ZB + zb) * SY + c * CY, TILE), CY)
                now = FA[1 + xl, zb, pl.ds(pl.multiple_of(TILE + c * CY, TILE), CY), :]
                FG[at, :] = now
                SRC[at, :] = BD[at, :] - W[at, :] * now

    def sweep(par, started=True, fresh=None, final=False):
        new = 1 - par

        @pl.loop(0, NC)
        def _(k):
            c = jnp.where(k == 0, 0, jnp.where(k == 1, NC - 1, k - 1))
            first, last = k == 0, k == 1

            @pl.when(first)
            def _():
                @pl.when(has_down)
                def _():
                    y_copy(1, par).wait_recv()

                unpack_y(par, 0)

            @pl.when(last)
            def _():
                @pl.when(has_up)
                def _():
                    y_copy(0, par).wait_recv()

                unpack_y(par, 1)

            if fresh is not None:
                @pl.when(fresh)
                def _():
                    next_source(c)

            at_each(gets_x, lambda way: x_copy(way, par, c).wait_recv())

            @pl.when(started)
            def _():
                at_each(sends_x, lambda way: x_copy(way, new, c).wait_send())

            @pl.loop(0, CY // TILE)
            def _(i):
                planes(par, c * CY + i * TILE, 1, 2, final)
                planes(par, c * CY + i * TILE, SX, SX + 1, final)

            if not final:
                at_each(sends_x, lambda way: x_copy(way, new, c).start())

            @pl.loop(0, CY // TILE)
            def _(i):
                planes(par, c * CY + i * TILE, 2, SX, final)

            def send_y(way):
                @pl.when(started)
                def _():
                    y_copy(way, new).wait_send()

                if not final:
                    pack_y(new, way)
                    y_copy(way, new).start()

            @pl.when(first & has_down)
            def _():
                send_y(0)

            @pl.when(last & has_up)
            def _():
                send_y(1)

    @pl.loop(0, STEPS * SWEEPS // 2 - 1)
    def _(pair):
        sweep(0, started=pair > 0, fresh=pair == 2)

        @pl.when(pair == 0)
        def _():
            send_all(msgW_copy, 1, n_tool)

        @pl.when(pair == 1)
        def _():
            wait_arrivals(msgB_copy)
            split_rows(msgBr)
            scatter(to_rest)

        @pl.when(pair == 2)
        def _():
            collect_and_send(0)

        sweep(1)

        @pl.when(pair == 0)
        def _():
            send_all(msgB_copy, 1, n_tool)
            wait_arrivals(msgW_copy)
            split_rows(msgWr)
            scatter(to_weight)

    sweep(0)
    sweep(1, final=True)

    stores = [
        pltpu.make_async_copy(
            FG.at[pl.ds((xl * ZB + zb) * SY, SY), :],
            tool_out.at[xl, :, pl.ds(zb * LANES, LANES)],
            out_sem.at[xl, zb],
        )
        for xl in range(SX)
        for zb in range(ZB)
    ]
    for copy in stores:
        copy.start()
    collect_and_send(1)

    def contact_of(k):
        backr[k, t] = backs[k, t]
        wait_arrivals(back_copy[k])
        split_rows(backr.at[k])
        got = jnp.dot(PT[...], R[...], preferred_element_type=jnp.float32)
        return got[:, :LANES] + got[:, LANES:]

    flux = film[...] * (contact_of(0) - theta1[...])
    sigma = 1.0 - 0.4 * jnp.tanh(theta1[...])
    rate = base_rate[...] + sigma * (acc[:, :LANES] + acc[:, LANES:])
    shell_out[...] = theta1[...] + shell_step * (flux + sigma * rate)
    contact_out[...] = contact_of(1)

    wait_sends(meta_copy)
    wait_sends(msg1_copy)
    wait_sends(msgW_copy)
    wait_sends(msgB_copy)
    wait_sends(back_copy[0])
    wait_sends(back_copy[1])
    at_each(sends_x, lambda way: kx_copy(way).wait_send())
    at_each(sends_y, lambda way: ky_copy(way).wait_send())

    @pl.loop(0, NC)
    def _(c):
        at_each(sends_x, lambda way: x_copy(way, 1, c).wait_send())

    at_each(sends_y, lambda way: y_copy(way, 1).wait_send())

    for copy in stores:
        copy.wait()


MESH = pl.DeviceIdType.MESH


def on_device(n_tool, n_blank, tool_temp, material, conductivity, shell_temp, base_rate, film, contact_temp, pair_slab, pair_block, bead_ids, bead_gain):
    SX, SY, SZ = tool_temp.shape
    ZB = SZ // LANES
    NC = CHUNKS
    BLK = shell_temp.shape[0]
    beadrows = bead_ids.shape[0] // LANES
    slots = n_tool * CAP
    voxel_blocks = SX * SY * ZB
    f32, bf16, i32 = jnp.float32, jnp.bfloat16, jnp.int32
    V = pltpu.VMEM
    dma = pltpu.SemaphoreType.DMA
    scratch = [
        V((SX + 2, ZB, SY + 2 * TILE, LANES), f32),
        V((SX + 2, ZB, SY + 2 * TILE, LANES), f32),
        V((SX + 2, ZB, SY + 2 * TILE, LANES), f32),
        V((SX, ZB, SY, LANES), i32),
        V((SX + 1, ZB, SY, LANES), f32),
        V((SX, ZB, SY + TILE, LANES), f32),
        V((SX, ZB, SY, LANES), f32),
        V((SX, ZB, SY, LANES), f32),
        V((voxel_blocks, LANES), f32),
        V((voxel_blocks, LANES), f32),
        V((voxel_blocks, LANES), f32),
        V((voxel_blocks, LANES), f32),
        V((voxel_blocks, slots), bf16),
        V((slots, BLK), bf16),
        V((BLK, slots), bf16),
        V((BLK, 4 * LANES), bf16),
        V((slots, 2 * LANES), bf16),
        V((BLK, TILE * LANES), bf16),
        V((2 * LANES, TILE * LANES), bf16),
        V((BLK, 2 * LANES), f32),
        V((BLK, LANES), i32),
        V((BLK, LANES), i32),
        V((slots // LANES, TILE, LANES), i32),
        V((n_tool, TILE, LANES), i32),
        V((slots // LANES, LANES), i32),
        pltpu.SMEM((slots // LANES, LANES), i32),
        V((2, 2, ZB, SX, LANES), f32),
        V((2, 2, ZB, SX, LANES), f32),
        V((2, ZB, SX, LANES), f32),
        V((2, ZB, SX, LANES), f32),
        V((n_tool, CAP, LANES), f32),
        V((n_tool, CAP, LANES), f32),
        V((n_tool, CAP, LANES), f32),
        V((n_tool, CAP, LANES), f32),
        V((n_tool, CAP, LANES), f32),
        V((n_tool, CAP, LANES), f32),
        V((STEPS, n_tool, CAP, LANES), f32),
        V((STEPS, n_tool, CAP, LANES), f32),
        V((BLK, LANES), f32),
        dma((2, ZB)),
        dma((SX, ZB)),
        dma,
        dma((2, 2, NC)),
        dma((2, 2, NC)),
        dma((2, 2)),
        dma((2, 2)),
        dma((2, 2)),
        dma((2, 2)),
        dma((n_tool,)),
        dma((n_tool,)),
        dma((n_tool,)),
        dma((n_tool,)),
        dma((n_tool,)),
        dma((n_tool,)),
        dma((n_tool,)),
        dma((n_tool,)),
        dma((STEPS, n_tool)),
        dma((STEPS, n_tool)),
    ]
    whole = pl.BlockSpec(memory_space=pltpu.VMEM)
    far = pl.BlockSpec(memory_space=pl.ANY)
    results = pl.pallas_call(
        functools.partial(kernel, (n_tool, n_blank, SX, SY, ZB, BLK, beadrows)),
        out_shape=(
            jax.ShapeDtypeStruct(tool_temp.shape, f32),
            jax.ShapeDtypeStruct(shell_temp.shape, f32),
            jax.ShapeDtypeStruct(shell_temp.shape, f32),
        ),
        in_specs=[far, far, pl.BlockSpec(memory_space=pltpu.SMEM)] + [whole] * 8,
        out_specs=(far, whole, whole),
        scratch_shapes=scratch,
        compiler_params=pltpu.CompilerParams(
            collective_id=0, has_side_effects=True, vmem_limit_bytes=60 * 2**20
        ),
    )(
        tool_temp,
        material,
        conductivity,
        shell_temp,
        base_rate,
        film,
        contact_temp,
        pair_slab.reshape(BLK // LANES, LANES),
        pair_block.reshape(BLK // LANES, LANES),
        bead_ids.reshape(beadrows, LANES),
        bead_gain.reshape(beadrows, LANES),
    )

    return pl.pallas_call(
        write_out,
        out_shape=tuple(jax.ShapeDtypeStruct(r.shape, r.dtype) for r in results),
        in_specs=[far] * 3,
        out_specs=(far,) * 3,
        scratch_shapes=[V(r.shape, f32) for r in results] + [dma((SX + 2,)), dma((SX + 2,))],
        compiler_params=pltpu.CompilerParams(vmem_limit_bytes=60 * 2**20),
    )(*results)


def write_out(tool_in, shell_in, contact_in, tool_out, shell_out, contact_out, tool_held, shell_held, contact_held, in_sems, out_sems):
    n = tool_in.shape[0]
    parts = [(tool_in.at[i], tool_held.at[i], tool_out.at[i]) for i in range(n)]
    parts += [(shell_in, shell_held, shell_out), (contact_in, contact_held, contact_out)]
    reads = [pltpu.make_async_copy(src, held, in_sems.at[i]) for i, (src, held, _) in enumerate(parts)]
    writes = [pltpu.make_async_copy(held, dst, out_sems.at[i]) for i, (_, held, dst) in enumerate(parts)]
    for copy in reads:
        copy.start()
    for read, write in zip(reads, writes):
        read.wait()
        write.start()
    for copy in writes:
        copy.wait()


def solution(mesh):
    placed = (
        P("tool", "blank", None),
        P("tool", "blank", None),
        P(),
        P(("blank", "tool"), None),
        P(("blank", "tool"), None),
        P(("blank", "tool"), None),
        P(("blank", "tool"), None),
        P(("blank", "tool"), None),
        P(("blank", "tool")),
        P(("blank", "tool")),
        P(("blank", "tool")),
    )
    return jax.shard_map(
        functools.partial(on_device, mesh.shape["tool"], mesh.shape["blank"]),
        mesh=mesh,
        in_specs=placed,
        out_specs=(
            P("tool", "blank", None),
            P(("blank", "tool"), None),
            P(("blank", "tool"), None),
        ),
        check_vma=False,
    )
```

```python
import functools
import math

import jax
import jax.numpy as jnp
from jax import lax
from jax.experimental import pallas as pl
from jax.experimental.pallas import tpu as pltpu
from jax.sharding import PartitionSpec as P

STEPS = 2
SWEEPS = 4
CAP = 64
LANES = 128
TILE = 8
CHUNKS = 4

diffuse_step = 0.12
source_step = 0.25
shell_step = 0.5
face_step = 0.5 * diffuse_step


def split_pair(x):
    hi = x.astype(jnp.bfloat16)
    lo = (x - hi.astype(jnp.float32)).astype(jnp.bfloat16)
    return hi, lo


def one_hot(mask):
    return jnp.where(mask, 1.0, 0.0).astype(jnp.bfloat16)


def fold_rows(acc):
    for shift in (4, 2, 1):
        acc = acc + pltpu.roll(acc, shift, 0)
    return acc


def column_of(row):
    return jnp.transpose(jnp.broadcast_to(row, (LANES, LANES)))


def kernel(
    dims,
    tool_hbm,
    mat_hbm,
    cond_hbm,
    theta0_hbm,
    base_hbm,
    film_hbm,
    contact_hbm,
    slab_hbm,
    block_hbm,
    bead_hbm,
    gain_hbm,
    tool_out,
    shell_out,
    contact_out,
    cond,
    theta0,
    base_rate,
    film,
    contact,
    slab_rows,
    block_rows,
    bead_rows,
    gain_rows,
    shell_end,
    contact_end,
    FA,
    FB,
    K,
    mat,
    Gx,
    Gy,
    GzH,
    GzL,
    SRC,
    W,
    BD,
    FG,
    O,
    PM,
    PT,
    XB,
    R,
    A,
    BT,
    acc,
    slot_col,
    lin_col,
    metas,
    metar,
    gidx_v,
    gidx_s,
    ys,
    yr,
    kys,
    kyr,
    msg1s,
    msg1r,
    msgWs,
    msgWr,
    msgBs,
    msgBr,
    backs,
    backr,
    theta1,
    in_sem,
    load_sem,
    out_sem,
    end_sem,
    idx_sem,
    xss,
    xrs,
    yss,
    yrs,
    kss,
    krs,
    metass,
    metars,
    m1ss,
    m1rs,
    mWss,
    mWrs,
    mBss,
    mBrs,
    bss,
    brs,
):
    n_tool, n_blank, SX, SY, ZB, BLK, BEADROWS = dims
    slots = n_tool * CAP
    voxel_blocks = SX * SY * ZB
    NC = CHUNKS
    CY = SY // NC
    F = (FA, FB)
    groups = BLK // LANES
    qgroups = slots // LANES
    t = lax.axis_index("tool")
    b = lax.axis_index("blank")
    has_left, has_right = t > 0, t < n_tool - 1
    has_down, has_up = b > 0, b < n_blank - 1

    barrier = pltpu.get_barrier_semaphore()

    @pl.loop(1, n_tool)
    def _(off):
        pl.semaphore_signal(
            barrier, inc=1, device_id={"tool": lax.rem(t + off, n_tool)}, device_id_type=MESH
        )

    @pl.when(has_down)
    def _():
        pl.semaphore_signal(barrier, inc=1, device_id={"blank": b - 1}, device_id_type=MESH)

    @pl.when(has_up)
    def _():
        pl.semaphore_signal(barrier, inc=1, device_id={"blank": b + 1}, device_id_type=MESH)

    small = [
        pltpu.make_async_copy(src, dst, in_sem.at[i])
        for i, (src, dst) in enumerate(
            (
                (slab_hbm, slab_rows),
                (block_hbm, block_rows),
                (film_hbm, film),
                (theta0_hbm, theta0),
                (contact_hbm, contact),
                (cond_hbm, cond),
                (base_hbm, base_rate),
                (bead_hbm, bead_rows),
                (gain_hbm, gain_rows),
            )
        )
    ]
    loads = []
    for zb in range(ZB):
        loads.append(
            pltpu.make_async_copy(
                mat_hbm.at[:, :, pl.ds(zb * LANES, LANES)],
                mat.at[:, zb],
                load_sem.at[1, zb],
            )
        )
    for zb in range(ZB):
        loads.append(
            pltpu.make_async_copy(
                tool_hbm.at[:, :, pl.ds(zb * LANES, LANES)],
                FA.at[pl.ds(1, SX), zb, pl.ds(TILE, SY), :],
                load_sem.at[0, zb],
            )
        )

    for copy in small[:6] + loads + small[6:]:
        copy.start()

    def clear_plane(plane):
        @pl.loop(0, ZB)
        def _(zb):
            zeros = jnp.zeros((SY, LANES), jnp.float32)
            K[plane, zb, pl.ds(TILE, SY), :] = zeros
            FA[plane, zb, pl.ds(TILE, SY), :] = zeros
            FB[plane, zb, pl.ds(TILE, SY), :] = zeros

    @pl.when(jnp.logical_not(has_left))
    def _():
        clear_plane(0)

    @pl.when(jnp.logical_not(has_right))
    def _():
        clear_plane(SX + 1)

    def clear_rim(side):
        zeros = jnp.zeros((ZB, SX, LANES), jnp.float32)
        yr[0, side] = zeros
        yr[1, side] = zeros
        kyr[side] = zeros

    @pl.when(jnp.logical_not(has_down))
    def _():
        clear_rim(0)

    @pl.when(jnp.logical_not(has_up))
    def _():
        clear_rim(1)

    sub8 = lax.broadcasted_iota(jnp.int32, (TILE, LANES), 0)
    lane8 = lax.broadcasted_iota(jnp.int32, (TILE, LANES), 1)

    def row8(ref, g):
        return jnp.broadcast_to(ref[pl.ds(g, 1), :], (TILE, LANES))

    for copy in small[:2]:
        copy.wait()
    for g in range(groups):
        slot_col[pl.ds(g * LANES, LANES), :] = column_of(slab_rows[pl.ds(g, 1), :])
        blk = block_rows[pl.ds(g, 1), :]
        yl = (blk // ZB) % SY
        lin = ((blk // (ZB * SY)) * ZB + blk % ZB) * SY + yl
        lin_col[pl.ds(g * LANES, LANES), :] = column_of(lin)

    slot_rows = []
    for g in range(groups):
        mine = row8(slab_rows, g)

        def count(i, total, mine=mine, g=g):
            other = slot_col[pl.ds(pl.multiple_of(i * TILE, TILE), TILE), :]
            before = (sub8 + i * TILE) < (lane8 + g * LANES)
            return total + jnp.where((other == mine) & before, 1, 0)

        rank = fold_rows(
            lax.fori_loop(0, (g + 1) * LANES // TILE, count, jnp.zeros((TILE, LANES), jnp.int32))
        )
        slot_rows.append(mine * CAP + rank)
    for g in range(groups):
        slot_col[pl.ds(g * LANES, LANES), :] = column_of(slot_rows[g][0:1])

    @pl.loop(0, slots // LANES)
    def _(i):
        rows = lax.broadcasted_iota(jnp.int32, (LANES, LANES), 0) + i * LANES
        for g in range(groups):
            PM[pl.ds(pl.multiple_of(i * LANES, LANES), LANES), g * LANES : (g + 1) * LANES] = one_hot(
                rows == jnp.broadcast_to(slot_rows[g][0:1], (LANES, LANES))
            )

    @pl.loop(0, qgroups)
    def _(q):
        def part(i, total):
            at = pl.ds(pl.multiple_of(i * 16, 16), 16)
            hit = slot_col[at, :] == (lax.broadcasted_iota(jnp.int32, (16, LANES), 1) + q * LANES)
            PT[at, pl.ds(pl.multiple_of(q * LANES, LANES), LANES)] = one_hot(hit)
            named = jnp.where(hit, lin_col[at, :] + 1, 0)
            return total + named[:TILE] + named[TILE:]

        total = lax.fori_loop(0, BLK // 16, part, jnp.zeros((TILE, LANES), jnp.int32), unroll=4)
        metas[q] = fold_rows(total) - 1

    for copy in small[2:5]:
        copy.wait()
    outflow = film[...] * (theta0[...] - contact[...])
    hi, lo = split_pair(outflow)
    XB[:, 0:LANES] = hi
    XB[:, LANES : 2 * LANES] = lo
    part_rows = min(512, slots)
    step_rows = min(512, voxel_blocks)

    def pack(write):
        @pl.loop(0, slots // part_rows)
        def _(i):
            got = jnp.dot(
                PM[pl.ds(pl.multiple_of(i * part_rows, part_rows), part_rows), :],
                XB[...],
                preferred_element_type=jnp.float32,
            )
            rows = got[:, :LANES] + got[:, LANES:]
            write(i * (part_rows // CAP), rows.reshape(part_rows // CAP, CAP, LANES))

    def write1(d, rows):
        msg1s[pl.ds(d, part_rows // CAP)] = rows

    pack(write1)

    pl.semaphore_wait(barrier, n_tool - 1 + jnp.where(has_down, 1, 0) + jnp.where(has_up, 1, 0))

    side = math.isqrt(n_tool)
    row, column = t // side, lax.rem(t, side)

    def partner(k):
        step = lax.rem(k * 7, n_tool)
        return lax.rem(row + step // side, side) * side + lax.rem(column + lax.rem(step, side), side)

    def source_of(k):
        step = lax.rem(k * 7, n_tool)
        return lax.rem(row + side - step // side, side) * side + lax.rem(column + side - lax.rem(step, side), side)

    def meta_copy(d, s):
        return pltpu.make_async_remote_copy(
            src_ref=metas.at[d // 2],
            dst_ref=metar.at[s],
            send_sem=metass.at[d],
            recv_sem=metars.at[s],
            device_id={"tool": d},
            device_id_type=MESH,
        )

    def row_copy(src, dst, ssem, rsem):
        def make(d, s):
            return pltpu.make_async_remote_copy(
                src_ref=src.at[d],
                dst_ref=dst.at[s],
                send_sem=ssem.at[d],
                recv_sem=rsem.at[s],
                device_id={"tool": d},
                device_id_type=MESH,
            )

        return make

    msg1_copy = row_copy(msg1s, msg1r, m1ss, m1rs)
    msgW_copy = row_copy(msgWs, msgWr, mWss, mWrs)
    msgB_copy = row_copy(msgBs, msgBr, mBss, mBrs)
    back_copy = [
        row_copy(backs.at[k], backr.at[k], bss.at[k], brs.at[k]) for k in range(STEPS)
    ]

    def send_all(make, first, last):
        @pl.loop(first, last)
        def _(off):
            make(partner(off), t).start()

    def wait_arrivals(make):
        @pl.loop(1, n_tool)
        def _(off):
            make(partner(off), source_of(off)).wait_recv()

    def wait_sends(make):
        @pl.loop(1, n_tool)
        def _(off):
            make(partner(off), t).wait_send()

    left = {"tool": jnp.where(has_left, t - 1, t + 1)}
    right = {"tool": jnp.where(has_right, t + 1, t - 1)}
    down = {"blank": jnp.where(has_down, b - 1, b + 1)}
    up = {"blank": jnp.where(has_up, b + 1, b - 1)}

    def x_copy(way, par, c):
        rows = pl.ds(pl.multiple_of(TILE + c * CY, TILE), CY)
        src, dst = (1, SX + 1) if way == 0 else (SX, 0)
        return pltpu.make_async_remote_copy(
            src_ref=F[par].at[src, :, rows, :],
            dst_ref=F[par].at[dst, :, rows, :],
            send_sem=xss.at[par, way, c],
            recv_sem=xrs.at[par, way, c],
            device_id=left if way == 0 else right,
            device_id_type=MESH,
        )

    def y_copy(way, par):
        return pltpu.make_async_remote_copy(
            src_ref=ys.at[par, way],
            dst_ref=yr.at[par, 1 - way],
            send_sem=yss.at[par, way],
            recv_sem=yrs.at[par, way],
            device_id=down if way == 0 else up,
            device_id_type=MESH,
        )

    def kx_copy(way):
        rows = pl.ds(TILE, SY)
        src, dst = (1, SX + 1) if way == 0 else (SX, 0)
        return pltpu.make_async_remote_copy(
            src_ref=K.at[src, :, rows, :],
            dst_ref=K.at[dst, :, rows, :],
            send_sem=kss.at[0, way],
            recv_sem=krs.at[0, way],
            device_id=left if way == 0 else right,
            device_id_type=MESH,
        )

    def ky_copy(way):
        return pltpu.make_async_remote_copy(
            src_ref=kys.at[way],
            dst_ref=kyr.at[1 - way],
            send_sem=kss.at[1, way],
            recv_sem=krs.at[1, way],
            device_id=down if way == 0 else up,
            device_id_type=MESH,
        )

    sends_x, sends_y = (has_left, has_right), (has_down, has_up)
    gets_x, gets_y = (has_right, has_left), (has_up, has_down)

    def at_each(flags, act):
        for way in range(2):
            @pl.when(flags[way])
            def _(way=way):
                act(way)

    send_all(meta_copy, 1, n_tool)
    send_all(msg1_copy, 1, n_tool)
    metar[t] = metas[t // 2]
    msg1r[t] = msg1s[t]

    small[5].wait()
    for zb in range(ZB):
        loads[zb].wait()

    @pl.loop(0, SX)
    def _(xl):
        @pl.loop(0, ZB)
        def _(zb):
            m = mat[xl, zb]
            low, mid, top = (m & 1) != 0, (m & 2) != 0, (m & 4) != 0
            pairs = [jnp.where(low, cond[2 * i + 1], cond[2 * i]) for i in range(4)]
            quads = [jnp.where(mid, pairs[2 * i + 1], pairs[2 * i]) for i in range(2)]
            K[1 + xl, zb, pl.ds(TILE, SY), :] = jnp.where(top, quads[1], quads[0])

    at_each(sends_x, lambda way: kx_copy(way).start())

    @pl.loop(0, ZB)
    def _(zb):
        for xl in range(SX):
            kys[0, zb, pl.ds(xl, 1), :] = K[1 + xl, zb, pl.ds(TILE, 1), :]
            kys[1, zb, pl.ds(xl, 1), :] = K[1 + xl, zb, pl.ds(TILE + SY - 1, 1), :]

    at_each(sends_y, lambda way: ky_copy(way).start())

    def pack_y(par, way):
        row = TILE if way == 0 else TILE + SY - 1

        @pl.loop(0, ZB)
        def _(zb):
            for xl in range(SX):
                ys[par, way, zb, pl.ds(xl, 1), :] = F[par][1 + xl, zb, pl.ds(row, 1), :]

    def unpack_y(par, side):
        row = TILE - 1 if side == 0 else TILE + SY

        @pl.loop(0, ZB)
        def _(zb):
            for xl in range(SX):
                F[par][1 + xl, zb, pl.ds(row, 1), :] = yr[par, side, zb, pl.ds(xl, 1), :]

    for zb in range(ZB):
        loads[ZB + zb].wait()

    for way in range(2):
        pack_y(0, way)
    at_each(sends_y, lambda way: y_copy(way, 0).start())

    @pl.loop(0, NC)
    def _(c):
        at_each(sends_x, lambda way: x_copy(way, 0, c).start())

    lane = lax.broadcasted_iota(jnp.int32, (SY, LANES), 1)
    last_lane, first_lane = lane == LANES - 1, lane == 0

    @pl.loop(0, SX)
    def _(xl):
        line = [K[1 + xl, zb, pl.ds(TILE, SY), :] for zb in range(ZB)]
        ahead = [pltpu.roll(k, LANES - 1, 1) for k in line] + [jnp.zeros((SY, LANES), jnp.float32)]
        behind = [jnp.zeros((SY, LANES), jnp.float32)] + [pltpu.roll(k, 1, 1) for k in line]
        for zb in range(ZB):
            high = jnp.where(last_lane, ahead[zb + 1], ahead[zb])
            low = jnp.where(first_lane, behind[zb], behind[zb + 1])
            GzH[xl, zb] = face_step * (line[zb] + high)
            GzL[xl, zb] = face_step * (line[zb] + low)

    def x_faces(p):
        @pl.loop(0, ZB)
        def _(zb):
            Gx[p, zb] = face_step * (K[p, zb, pl.ds(TILE, SY), :] + K[p + 1, zb, pl.ds(TILE, SY), :])

    @pl.loop(1, SX)
    def _(p):
        x_faces(p)

    wait_arrivals(meta_copy)
    even = lax.rem(t, 2) == 0
    lin_rows = []
    for q in range(qgroups):
        first, second = metar[2 * q], metar[2 * q + 1]
        first = jnp.where(even, first, pltpu.roll(first, CAP, 1))
        second = jnp.where(even, pltpu.roll(second, CAP, 1), second)
        lin = jnp.where(lane8 < CAP, first, second)
        lin_rows.append(lin)
        gidx_v[pl.ds(q, 1), :] = jnp.maximum(lin[0:1], 0)
    to_smem = pltpu.make_async_copy(gidx_v, gidx_s, idx_sem)
    to_smem.start()

    @pl.loop(0, voxel_blocks // LANES)
    def _(i):
        rows = lax.broadcasted_iota(jnp.int32, (LANES, LANES), 0) + i * LANES
        for q in range(qgroups):
            O[pl.ds(pl.multiple_of(i * LANES, LANES), LANES), q * LANES : (q + 1) * LANES] = one_hot(
                rows == jnp.broadcast_to(lin_rows[q][0:1], (LANES, LANES))
            )

    to_smem.wait()

    at_each(gets_y, lambda way: ky_copy(way).wait_recv())

    @pl.loop(0, ZB)
    def _(zb):
        for xl in range(SX):
            K[1 + xl, zb, pl.ds(TILE - 1, 1), :] = kyr[0, zb, pl.ds(xl, 1), :]
            K[1 + xl, zb, pl.ds(TILE + SY, 1), :] = kyr[1, zb, pl.ds(xl, 1), :]

    @pl.loop(0, SX)
    def _(xl):
        @pl.loop(0, ZB)
        def _(zb):
            Gy[xl, zb, pl.ds(TILE - 1, 1), :] = face_step * (
                K[1 + xl, zb, pl.ds(TILE - 1, 1), :] + K[1 + xl, zb, pl.ds(TILE, 1), :]
            )
            Gy[xl, zb, pl.ds(TILE, SY), :] = face_step * (
                K[1 + xl, zb, pl.ds(TILE, SY), :] + K[1 + xl, zb, pl.ds(TILE + 1, SY), :]
            )

    def split_rows(src):
        @pl.loop(0, n_tool)
        def _(s):
            hi, lo = split_pair(src[s])
            at = pl.ds(pl.multiple_of(s * CAP, CAP), CAP)
            R[at, 0:LANES] = hi
            R[at, LANES : 2 * LANES] = lo

    def scatter(write):
        @pl.loop(0, voxel_blocks // step_rows)
        def _(m):
            at = pl.ds(pl.multiple_of(m * step_rows, step_rows), step_rows)
            got = jnp.dot(
                O[at, :], R[...], preferred_element_type=jnp.float32
            )
            write(at, source_step * (got[:, :LANES] + got[:, LANES:]))

    def to_source(at, rows):
        SRC[at, :] = rows

    def to_weight(at, rows):
        W[at, :] = rows

    def to_rest(at, rows):
        BD[at, :] = rows

    wait_arrivals(msg1_copy)
    split_rows(msg1r)
    scatter(to_source)

    at_each(gets_x, lambda way: kx_copy(way).wait_recv())
    x_faces(0)
    x_faces(SX)

    def add_gains():
        for copy in small[7:]:
            copy.wait()
        for j in range(BEADROWS // TILE):
            @pl.loop(0, TILE)
            def _(i, j=j):
                at = pl.ds(pl.multiple_of(i * LANES, LANES), LANES)
                shell = bead_rows[pl.ds(j * TILE + i, 1), :]
                row, lane = shell // LANES, shell % LANES
                A[:, at] = one_hot(
                    lax.broadcasted_iota(jnp.int32, (BLK, LANES), 0) == jnp.broadcast_to(row, (BLK, LANES))
                )
                here = lax.broadcasted_iota(jnp.int32, (LANES, LANES), 0) == jnp.broadcast_to(lane, (LANES, LANES))
                held = jnp.where(here, jnp.broadcast_to(gain_rows[pl.ds(j * TILE + i, 1), :], (LANES, LANES)), 0.0)
                hi, lo = split_pair(held)
                BT[0:LANES, at] = hi
                BT[LANES : 2 * LANES, at] = lo

            part = lax.dot_general(
                A[...], BT[...], (((1,), (1,)), ((), ())), preferred_element_type=jnp.float32
            )
            if j == 0:
                acc[...] = part
            else:
                acc[...] += part

    def pack_pair(rows, out):
        hi, lo = split_pair(rows)
        XB[:, 0:LANES] = hi
        XB[:, LANES : 2 * LANES] = lo

        def write(d, rows):
            out[pl.ds(d, part_rows // CAP)] = rows

        pack(write)

    def shells_after_first():
        small[6].wait()
        sigma = 1.0 - 0.4 * jnp.tanh(theta0[...])
        rate = base_rate[...] + sigma * (acc[:, :LANES] + acc[:, LANES:])
        outflow = film[...] * (theta0[...] - contact[...])
        theta1[...] = theta0[...] + shell_step * (sigma * rate - outflow)

    lane_t = lax.broadcasted_iota(jnp.int32, (TILE, LANES), 1)
    top_lane, low_lane = lane_t == LANES - 1, lane_t == 0
    no_heat = jnp.zeros((TILE, LANES), jnp.float32)

    def planes(par, y0, first, last, final):
        old, new = F[par], F[1 - par]
        y0 = pl.multiple_of(y0, TILE)
        rows = pl.ds(pl.multiple_of(y0 + TILE, TILE), TILE)
        all_z = range(ZB)

        def temp(p, zb, shift=0):
            return old[p, zb, rows if shift == 0 else pl.ds(y0 + TILE + shift, TILE), :]

        center = [temp(first, zb) for zb in all_z]
        below = [Gx[first - 1, zb, pl.ds(y0, TILE), :] * (center[zb] - temp(first - 1, zb)) for zb in all_z]
        for p in range(first, last):
            xl = p - 1
            ahead = [temp(p + 1, zb) for zb in all_z]
            above = [Gx[p, zb, pl.ds(y0, TILE), :] * (ahead[zb] - center[zb]) for zb in all_z]
            after = [pltpu.roll(now, LANES - 1, 1) for now in center] + [no_heat]
            before = [no_heat] + [pltpu.roll(now, 1, 1) for now in center]
            for zb in all_z:
                now = center[zb]
                z_high = GzH[xl, zb, pl.ds(y0, TILE), :] * (jnp.where(top_lane, after[zb + 1], after[zb]) - now)
                z_low = GzL[xl, zb, pl.ds(y0, TILE), :] * (now - jnp.where(low_lane, before[zb], before[zb + 1]))
                y_high = Gy[xl, zb, rows, :] * (temp(p, zb, 1) - now)
                y_low = Gy[xl, zb, pl.ds(y0 + TILE - 1, TILE), :] * (now - temp(p, zb, -1))
                at = pl.multiple_of((xl * ZB + zb) * SY + y0, TILE)
                total = (above[zb] - below[zb]) + (y_high - y_low) + (z_high - z_low)
                result = now + (total + SRC[pl.ds(at, TILE), :])
                if final:
                    FG[pl.ds(at, TILE), :] = result
                else:
                    new[p, zb, rows, :] = result
            center, below = ahead, above

    def collect(k, d):
        q = d // 2
        lane0 = lax.rem(d, 2) * CAP

        @pl.loop(0, CAP // TILE)
        def _(j):
            for i in range(TILE):
                row = gidx_s[q, lane0 + j * TILE + i]
                backs[k, d, pl.ds(pl.multiple_of(j * TILE, TILE) + i, 1), :] = FG[pl.ds(row, 1), :]

    def collect_and_send(k, first, last):
        @pl.loop(first, last)
        def _(off):
            d = partner(off)
            collect(k, d)
            back_copy[k](d, t).start()

    def next_source(c):
        @pl.loop(0, SX)
        def _(xl):
            for zb in range(ZB):
                at = pl.ds(pl.multiple_of((xl * ZB + zb) * SY + c * CY, TILE), CY)
                now = FA[1 + xl, zb, pl.ds(pl.multiple_of(TILE + c * CY, TILE), CY), :]
                FG[at, :] = now
                SRC[at, :] = BD[at, :] - W[at, :] * now

    def sweep(par, started=True, fresh=None, final=False):
        new = 1 - par

        @pl.loop(0, NC)
        def _(k):
            c = jnp.where(k == 0, 0, jnp.where(k == 1, NC - 1, k - 1))
            first, last = k == 0, k == 1

            @pl.when(first)
            def _():
                @pl.when(has_down)
                def _():
                    y_copy(1, par).wait_recv()

                unpack_y(par, 0)

            @pl.when(last)
            def _():
                @pl.when(has_up)
                def _():
                    y_copy(0, par).wait_recv()

                unpack_y(par, 1)

            if fresh is not None:
                @pl.when(fresh)
                def _():
                    next_source(c)

            at_each(gets_x, lambda way: x_copy(way, par, c).wait_recv())

            @pl.when(started)
            def _():
                at_each(sends_x, lambda way: x_copy(way, new, c).wait_send())

            @pl.loop(0, CY // TILE)
            def _(i):
                planes(par, c * CY + i * TILE, 1, 2, final)
                planes(par, c * CY + i * TILE, SX, SX + 1, final)

            if not final:
                at_each(sends_x, lambda way: x_copy(way, new, c).start())

            @pl.loop(0, CY // TILE)
            def _(i):
                planes(par, c * CY + i * TILE, 2, SX, final)

            def send_y(way):
                @pl.when(started)
                def _():
                    y_copy(way, new).wait_send()

                if not final:
                    pack_y(new, way)
                    y_copy(way, new).start()

            @pl.when(first & has_down)
            def _():
                send_y(0)

            @pl.when(last & has_up)
            def _():
                send_y(1)

    @pl.loop(0, STEPS * SWEEPS // 2 - 1)
    def _(pair):
        sweep(0, started=pair > 0, fresh=pair == 2)

        @pl.when(pair == 0)
        def _():
            pack_pair(film[...], msgWs)
            send_all(msgW_copy, 1, n_tool)
            msgWr[t] = msgWs[t]
            add_gains()

        @pl.when(pair == 1)
        def _():
            wait_arrivals(msgW_copy)
            split_rows(msgWr)
            scatter(to_weight)

        @pl.when(pair == 2)
        def _():
            collect_and_send(0, 1, n_tool // 3 + 1)
            collect(0, t)

        sweep(1)

        @pl.when(pair == 2)
        def _():
            collect_and_send(0, n_tool // 3 + 1, 2 * n_tool // 3 + 1)

        @pl.when(pair == 1)
        def _():
            wait_arrivals(msgB_copy)
            split_rows(msgBr)
            scatter(to_rest)

        @pl.when(pair == 0)
        def _():
            shells_after_first()
            pack_pair(film[...] * theta1[...], msgBs)
            send_all(msgB_copy, 1, n_tool)
            msgBr[t] = msgBs[t]

    sweep(0)
    collect_and_send(0, 2 * n_tool // 3 + 1, n_tool)
    sweep(1, final=True)

    stores = [
        pltpu.make_async_copy(
            FG.at[pl.ds((xl * ZB + zb) * SY, SY), :],
            tool_out.at[xl, :, pl.ds(zb * LANES, LANES)],
            out_sem.at[xl, zb],
        )
        for xl in range(SX)
        for zb in range(ZB)
    ]
    collect_and_send(1, 1, n_tool)
    collect(1, t)
    for copy in stores:
        copy.start()

    def contact_of(k):
        backr[k, t] = backs[k, t]
        wait_arrivals(back_copy[k])
        split_rows(backr.at[k])
        got = jnp.dot(PT[...], R[...], preferred_element_type=jnp.float32)
        return got[:, :LANES] + got[:, LANES:]

    flux = film[...] * (contact_of(0) - theta1[...])
    sigma = 1.0 - 0.4 * jnp.tanh(theta1[...])
    rate = base_rate[...] + sigma * (acc[:, :LANES] + acc[:, LANES:])
    shell_end[...] = theta1[...] + shell_step * (flux + sigma * rate)
    stores.append(pltpu.make_async_copy(shell_end, shell_out, end_sem.at[0]))
    stores[-1].start()
    contact_end[...] = contact_of(1)
    stores.append(pltpu.make_async_copy(contact_end, contact_out, end_sem.at[1]))
    stores[-1].start()

    wait_sends(meta_copy)
    wait_sends(msg1_copy)
    wait_sends(msgW_copy)
    wait_sends(msgB_copy)
    wait_sends(back_copy[0])
    wait_sends(back_copy[1])
    at_each(sends_x, lambda way: kx_copy(way).wait_send())
    at_each(sends_y, lambda way: ky_copy(way).wait_send())

    @pl.loop(0, NC)
    def _(c):
        at_each(sends_x, lambda way: x_copy(way, 1, c).wait_send())

    at_each(sends_y, lambda way: y_copy(way, 1).wait_send())

    for copy in stores:
        copy.wait()


MESH = pl.DeviceIdType.MESH


def on_device(n_tool, n_blank, tool_temp, material, conductivity, shell_temp, base_rate, film, contact_temp, pair_slab, pair_block, bead_ids, bead_gain):
    SX, SY, SZ = tool_temp.shape
    ZB = SZ // LANES
    NC = CHUNKS
    BLK = shell_temp.shape[0]
    beadrows = bead_ids.shape[0] // LANES
    slots = n_tool * CAP
    voxel_blocks = SX * SY * ZB
    f32, bf16, i32 = jnp.float32, jnp.bfloat16, jnp.int32
    V = pltpu.VMEM
    dma = pltpu.SemaphoreType.DMA
    scratch = [
        pltpu.SMEM(conductivity.shape, f32),
        V((BLK, LANES), f32),
        V((BLK, LANES), f32),
        V((BLK, LANES), f32),
        V((BLK, LANES), f32),
        V((BLK // LANES, LANES), i32),
        V((BLK // LANES, LANES), i32),
        V((beadrows, LANES), i32),
        V((beadrows, LANES), f32),
        V((BLK, LANES), f32),
        V((BLK, LANES), f32),
        V((SX + 2, ZB, SY + 2 * TILE, LANES), f32),
        V((SX + 2, ZB, SY + 2 * TILE, LANES), f32),
        V((SX + 2, ZB, SY + 2 * TILE, LANES), f32),
        V((SX, ZB, SY, LANES), i32),
        V((SX + 1, ZB, SY, LANES), f32),
        V((SX, ZB, SY + TILE, LANES), f32),
        V((SX, ZB, SY, LANES), f32),
        V((SX, ZB, SY, LANES), f32),
        V((voxel_blocks, LANES), f32),
        V((voxel_blocks, LANES), f32),
        V((voxel_blocks, LANES), f32),
        V((voxel_blocks, LANES), f32),
        V((voxel_blocks, slots), bf16),
        V((slots, BLK), bf16),
        V((BLK, slots), bf16),
        V((BLK, 2 * LANES), bf16),
        V((slots, 2 * LANES), bf16),
        V((BLK, TILE * LANES), bf16),
        V((2 * LANES, TILE * LANES), bf16),
        V((BLK, 2 * LANES), f32),
        V((BLK, LANES), i32),
        V((BLK, LANES), i32),
        V((slots // LANES, TILE, LANES), i32),
        V((n_tool, TILE, LANES), i32),
        V((slots // LANES, LANES), i32),
        pltpu.SMEM((slots // LANES, LANES), i32),
        V((2, 2, ZB, SX, LANES), f32),
        V((2, 2, ZB, SX, LANES), f32),
        V((2, ZB, SX, LANES), f32),
        V((2, ZB, SX, LANES), f32),
        V((n_tool, CAP, LANES), f32),
        V((n_tool, CAP, LANES), f32),
        V((n_tool, CAP, LANES), f32),
        V((n_tool, CAP, LANES), f32),
        V((n_tool, CAP, LANES), f32),
        V((n_tool, CAP, LANES), f32),
        V((STEPS, n_tool, CAP, LANES), f32),
        V((STEPS, n_tool, CAP, LANES), f32),
        V((BLK, LANES), f32),
        dma((9,)),
        dma((2, ZB)),
        dma((SX, ZB)),
        dma((2,)),
        dma,
        dma((2, 2, NC)),
        dma((2, 2, NC)),
        dma((2, 2)),
        dma((2, 2)),
        dma((2, 2)),
        dma((2, 2)),
        dma((n_tool,)),
        dma((n_tool,)),
        dma((n_tool,)),
        dma((n_tool,)),
        dma((n_tool,)),
        dma((n_tool,)),
        dma((n_tool,)),
        dma((n_tool,)),
        dma((STEPS, n_tool)),
        dma((STEPS, n_tool)),
    ]
    far = pl.BlockSpec(memory_space=pl.ANY)
    results = pl.pallas_call(
        functools.partial(kernel, (n_tool, n_blank, SX, SY, ZB, BLK, beadrows)),
        out_shape=(
            jax.ShapeDtypeStruct(tool_temp.shape, f32),
            jax.ShapeDtypeStruct(shell_temp.shape, f32),
            jax.ShapeDtypeStruct(shell_temp.shape, f32),
        ),
        in_specs=[far] * 11,
        out_specs=(far,) * 3,
        scratch_shapes=scratch,
        compiler_params=pltpu.CompilerParams(
            collective_id=0, has_side_effects=True, vmem_limit_bytes=60 * 2**20
        ),
    )(
        tool_temp,
        material,
        conductivity,
        shell_temp,
        base_rate,
        film,
        contact_temp,
        pair_slab.reshape(BLK // LANES, LANES),
        pair_block.reshape(BLK // LANES, LANES),
        bead_ids.reshape(beadrows, LANES),
        bead_gain.reshape(beadrows, LANES),
    )

    return pl.pallas_call(
        write_out,
        out_shape=tuple(jax.ShapeDtypeStruct(r.shape, r.dtype) for r in results),
        in_specs=[far] * 3,
        out_specs=(far,) * 3,
        scratch_shapes=[V(r.shape, f32) for r in results] + [dma((SX + 2,)), dma((SX + 2,))],
        compiler_params=pltpu.CompilerParams(vmem_limit_bytes=60 * 2**20),
    )(*results)


def write_out(tool_in, shell_in, contact_in, tool_out, shell_out, contact_out, tool_held, shell_held, contact_held, in_sems, out_sems):
    n = tool_in.shape[0]
    parts = [(tool_in.at[i], tool_held.at[i], tool_out.at[i]) for i in range(n)]
    parts += [(shell_in, shell_held, shell_out), (contact_in, contact_held, contact_out)]
    reads = [pltpu.make_async_copy(src, held, in_sems.at[i]) for i, (src, held, _) in enumerate(parts)]
    writes = [pltpu.make_async_copy(held, dst, out_sems.at[i]) for i, (_, held, dst) in enumerate(parts)]
    for copy in reads:
        copy.start()
    for read, write in zip(reads, writes):
        read.wait()
        write.start()
    for copy in writes:
        copy.wait()


def solution(mesh):
    placed = (
        P("tool", "blank", None),
        P("tool", "blank", None),
        P(),
        P(("blank", "tool"), None),
        P(("blank", "tool"), None),
        P(("blank", "tool"), None),
        P(("blank", "tool"), None),
        P(("blank", "tool"), None),
        P(("blank", "tool")),
        P(("blank", "tool")),
        P(("blank", "tool")),
    )
    return jax.shard_map(
        functools.partial(on_device, mesh.shape["tool"], mesh.shape["blank"]),
        mesh=mesh,
        in_specs=placed,
        out_specs=(
            P("tool", "blank", None),
            P(("blank", "tool"), None),
            P(("blank", "tool"), None),
        ),
        check_vma=False,
    )
```

```python
import functools
import math

import jax
import jax.numpy as jnp
from jax import lax
from jax.experimental import pallas as pl
from jax.experimental.pallas import tpu as pltpu
from jax.sharding import PartitionSpec as P

STEPS = 2
SWEEPS = 4
CAP = 64
LANES = 128
TILE = 8
CHUNKS = 4

diffuse_step = 0.12
source_step = 0.25
shell_step = 0.5
face_step = 0.5 * diffuse_step


def split_pair(x):
    hi = x.astype(jnp.bfloat16)
    lo = (x - hi.astype(jnp.float32)).astype(jnp.bfloat16)
    return hi, lo


def one_hot(mask):
    return jnp.where(mask, 1.0, 0.0).astype(jnp.bfloat16)


def fold_rows(acc):
    for shift in (4, 2, 1):
        acc = acc + pltpu.roll(acc, shift, 0)
    return acc


def column_of(row):
    return jnp.transpose(jnp.broadcast_to(row, (LANES, LANES)))


def kernel(
    dims,
    tool_hbm,
    mat_hbm,
    cond_hbm,
    theta0_hbm,
    base_hbm,
    film_hbm,
    contact_hbm,
    slab_hbm,
    block_hbm,
    bead_hbm,
    gain_hbm,
    tool_out,
    shell_out,
    contact_out,
    cond,
    theta0,
    base_rate,
    film,
    contact,
    slab_rows,
    block_rows,
    bead_rows,
    gain_rows,
    shell_end,
    contact_end,
    FA,
    FB,
    K,
    mat,
    Gx,
    Gy,
    GzH,
    GzL,
    SRC,
    W,
    BD,
    FG,
    O,
    PM,
    PT,
    XB,
    R,
    A,
    BT,
    acc,
    slot_col,
    lin_col,
    metas,
    metar,
    gidx_v,
    gidx_s,
    ys,
    yr,
    kys,
    kyr,
    msg1s,
    msg1r,
    msgWs,
    msgWr,
    msgBs,
    msgBr,
    backs,
    backr,
    theta1,
    in_sem,
    load_sem,
    out_sem,
    end_sem,
    idx_sem,
    xss,
    xrs,
    yss,
    yrs,
    kss,
    krs,
    metass,
    metars,
    m1ss,
    m1rs,
    mWss,
    mWrs,
    mBss,
    mBrs,
    bss,
    brs,
):
    n_tool, n_blank, SX, SY, ZB, BLK, BEADROWS = dims
    slots = n_tool * CAP
    voxel_blocks = SX * SY * ZB
    NC = CHUNKS
    CY = SY // NC
    F = (FA, FB)
    groups = BLK // LANES
    qgroups = slots // LANES
    t = lax.axis_index("tool")
    b = lax.axis_index("blank")
    has_left, has_right = t > 0, t < n_tool - 1
    has_down, has_up = b > 0, b < n_blank - 1

    barrier = pltpu.get_barrier_semaphore()

    @pl.loop(1, n_tool)
    def _(off):
        pl.semaphore_signal(
            barrier, inc=1, device_id={"tool": lax.rem(t + off, n_tool)}, device_id_type=MESH
        )

    @pl.when(has_down)
    def _():
        pl.semaphore_signal(barrier, inc=1, device_id={"blank": b - 1}, device_id_type=MESH)

    @pl.when(has_up)
    def _():
        pl.semaphore_signal(barrier, inc=1, device_id={"blank": b + 1}, device_id_type=MESH)

    small = [
        pltpu.make_async_copy(src, dst, in_sem.at[i])
        for i, (src, dst) in enumerate(
            (
                (slab_hbm, slab_rows),
                (block_hbm, block_rows),
                (film_hbm, film),
                (theta0_hbm, theta0),
                (contact_hbm, contact),
                (cond_hbm, cond),
                (base_hbm, base_rate),
                (bead_hbm, bead_rows),
                (gain_hbm, gain_rows),
            )
        )
    ]
    loads = []
    for zb in range(ZB):
        loads.append(
            pltpu.make_async_copy(
                mat_hbm.at[:, :, pl.ds(zb * LANES, LANES)],
                mat.at[:, zb],
                load_sem.at[1, zb],
            )
        )
    for zb in range(ZB):
        loads.append(
            pltpu.make_async_copy(
                tool_hbm.at[:, :, pl.ds(zb * LANES, LANES)],
                FA.at[pl.ds(1, SX), zb, pl.ds(TILE, SY), :],
                load_sem.at[0, zb],
            )
        )

    for copy in small[:6] + loads + small[6:]:
        copy.start()

    def clear_plane(plane):
        @pl.loop(0, ZB)
        def _(zb):
            zeros = jnp.zeros((SY, LANES), jnp.float32)
            K[plane, zb, pl.ds(TILE, SY), :] = zeros
            FA[plane, zb, pl.ds(TILE, SY), :] = zeros
            FB[plane, zb, pl.ds(TILE, SY), :] = zeros

    @pl.when(jnp.logical_not(has_left))
    def _():
        clear_plane(0)

    @pl.when(jnp.logical_not(has_right))
    def _():
        clear_plane(SX + 1)

    def clear_rim(side):
        zeros = jnp.zeros((ZB, SX, LANES), jnp.float32)
        yr[0, side] = zeros
        yr[1, side] = zeros
        kyr[side] = zeros

    @pl.when(jnp.logical_not(has_down))
    def _():
        clear_rim(0)

    @pl.when(jnp.logical_not(has_up))
    def _():
        clear_rim(1)

    sub8 = lax.broadcasted_iota(jnp.int32, (TILE, LANES), 0)
    lane8 = lax.broadcasted_iota(jnp.int32, (TILE, LANES), 1)

    def row8(ref, g):
        return jnp.broadcast_to(ref[pl.ds(g, 1), :], (TILE, LANES))

    for copy in small[:2]:
        copy.wait()
    for g in range(groups):
        slot_col[pl.ds(g * LANES, LANES), :] = column_of(slab_rows[pl.ds(g, 1), :])
        blk = block_rows[pl.ds(g, 1), :]
        yl = (blk // ZB) % SY
        lin = ((blk // (ZB * SY)) * ZB + blk % ZB) * SY + yl
        lin_col[pl.ds(g * LANES, LANES), :] = column_of(lin)

    slot_rows = []
    for g in range(groups):
        mine = row8(slab_rows, g)

        def count(i, total, mine=mine, g=g):
            other = slot_col[pl.ds(pl.multiple_of(i * TILE, TILE), TILE), :]
            before = (sub8 + i * TILE) < (lane8 + g * LANES)
            return total + jnp.where((other == mine) & before, 1, 0)

        rank = fold_rows(
            lax.fori_loop(0, (g + 1) * LANES // TILE, count, jnp.zeros((TILE, LANES), jnp.int32))
        )
        slot_rows.append(mine * CAP + rank)
    for g in range(groups):
        slot_col[pl.ds(g * LANES, LANES), :] = column_of(slot_rows[g][0:1])

    @pl.loop(0, slots // LANES)
    def _(i):
        rows = lax.broadcasted_iota(jnp.int32, (LANES, LANES), 0) + i * LANES
        for g in range(groups):
            PM[pl.ds(pl.multiple_of(i * LANES, LANES), LANES), g * LANES : (g + 1) * LANES] = one_hot(
                rows == jnp.broadcast_to(slot_rows[g][0:1], (LANES, LANES))
            )

    @pl.loop(0, qgroups)
    def _(q):
        def part(i, total):
            at = pl.ds(pl.multiple_of(i * 16, 16), 16)
            hit = slot_col[at, :] == (lax.broadcasted_iota(jnp.int32, (16, LANES), 1) + q * LANES)
            PT[at, pl.ds(pl.multiple_of(q * LANES, LANES), LANES)] = one_hot(hit)
            named = jnp.where(hit, lin_col[at, :] + 1, 0)
            return total + named[:TILE] + named[TILE:]

        total = lax.fori_loop(0, BLK // 16, part, jnp.zeros((TILE, LANES), jnp.int32), unroll=4)
        metas[q] = fold_rows(total) - 1

    for copy in small[2:5]:
        copy.wait()
    outflow = film[...] * (theta0[...] - contact[...])
    hi, lo = split_pair(outflow)
    XB[:, 0:LANES] = hi
    XB[:, LANES : 2 * LANES] = lo
    part_rows = min(512, slots)
    step_rows = min(512, voxel_blocks)

    def pack(write):
        @pl.loop(0, slots // part_rows)
        def _(i):
            got = jnp.dot(
                PM[pl.ds(pl.multiple_of(i * part_rows, part_rows), part_rows), :],
                XB[...],
                preferred_element_type=jnp.float32,
            )
            rows = got[:, :LANES] + got[:, LANES:]
            write(i * (part_rows // CAP), rows.reshape(part_rows // CAP, CAP, LANES))

    def write1(d, rows):
        msg1s[pl.ds(d, part_rows // CAP)] = rows

    pack(write1)

    pl.semaphore_wait(barrier, n_tool - 1 + jnp.where(has_down, 1, 0) + jnp.where(has_up, 1, 0))

    side = math.isqrt(n_tool)
    row, column = t // side, lax.rem(t, side)

    def partner(k):
        step = k
        return lax.rem(row + step // side, side) * side + lax.rem(column + lax.rem(step, side), side)

    def source_of(k):
        step = k
        return lax.rem(row + side - step // side, side) * side + lax.rem(column + side - lax.rem(step, side), side)

    def meta_copy(d, s):
        return pltpu.make_async_remote_copy(
            src_ref=metas.at[d // 2],
            dst_ref=metar.at[s],
            send_sem=metass.at[d],
            recv_sem=metars.at[s],
            device_id={"tool": d},
            device_id_type=MESH,
        )

    def row_copy(src, dst, ssem, rsem):
        def make(d, s):
            return pltpu.make_async_remote_copy(
                src_ref=src.at[d],
                dst_ref=dst.at[s],
                send_sem=ssem.at[d],
                recv_sem=rsem.at[s],
                device_id={"tool": d},
                device_id_type=MESH,
            )

        return make

    msg1_copy = row_copy(msg1s, msg1r, m1ss, m1rs)
    msgW_copy = row_copy(msgWs, msgWr, mWss, mWrs)
    msgB_copy = row_copy(msgBs, msgBr, mBss, mBrs)
    back_copy = [
        row_copy(backs.at[k], backr.at[k], bss.at[k], brs.at[k]) for k in range(STEPS)
    ]

    def send_all(make, first, last):
        @pl.loop(first, last)
        def _(off):
            make(partner(off), t).start()

    def wait_arrivals(make):
        @pl.loop(1, n_tool)
        def _(off):
            make(partner(off), source_of(off)).wait_recv()

    def wait_sends(make):
        @pl.loop(1, n_tool)
        def _(off):
            make(partner(off), t).wait_send()

    left = {"tool": jnp.where(has_left, t - 1, t + 1)}
    right = {"tool": jnp.where(has_right, t + 1, t - 1)}
    down = {"blank": jnp.where(has_down, b - 1, b + 1)}
    up = {"blank": jnp.where(has_up, b + 1, b - 1)}

    def x_copy(way, par, c):
        rows = pl.ds(pl.multiple_of(TILE + c * CY, TILE), CY)
        src, dst = (1, SX + 1) if way == 0 else (SX, 0)
        return pltpu.make_async_remote_copy(
            src_ref=F[par].at[src, :, rows, :],
            dst_ref=F[par].at[dst, :, rows, :],
            send_sem=xss.at[par, way, c],
            recv_sem=xrs.at[par, way, c],
            device_id=left if way == 0 else right,
            device_id_type=MESH,
        )

    def y_copy(way, par):
        return pltpu.make_async_remote_copy(
            src_ref=ys.at[par, way],
            dst_ref=yr.at[par, 1 - way],
            send_sem=yss.at[par, way],
            recv_sem=yrs.at[par, way],
            device_id=down if way == 0 else up,
            device_id_type=MESH,
        )

    def kx_copy(way):
        rows = pl.ds(TILE, SY)
        src, dst = (1, SX + 1) if way == 0 else (SX, 0)
        return pltpu.make_async_remote_copy(
            src_ref=K.at[src, :, rows, :],
            dst_ref=K.at[dst, :, rows, :],
            send_sem=kss.at[0, way],
            recv_sem=krs.at[0, way],
            device_id=left if way == 0 else right,
            device_id_type=MESH,
        )

    def ky_copy(way):
        return pltpu.make_async_remote_copy(
            src_ref=kys.at[way],
            dst_ref=kyr.at[1 - way],
            send_sem=kss.at[1, way],
            recv_sem=krs.at[1, way],
            device_id=down if way == 0 else up,
            device_id_type=MESH,
        )

    sends_x, sends_y = (has_left, has_right), (has_down, has_up)
    gets_x, gets_y = (has_right, has_left), (has_up, has_down)

    def at_each(flags, act):
        for way in range(2):
            @pl.when(flags[way])
            def _(way=way):
                act(way)

    send_all(meta_copy, 1, n_tool)
    send_all(msg1_copy, 1, n_tool)
    metar[t] = metas[t // 2]
    msg1r[t] = msg1s[t]

    small[5].wait()
    for zb in range(ZB):
        loads[zb].wait()

    @pl.loop(0, SX)
    def _(xl):
        @pl.loop(0, ZB)
        def _(zb):
            m = mat[xl, zb]
            low, mid, top = (m & 1) != 0, (m & 2) != 0, (m & 4) != 0
            pairs = [jnp.where(low, cond[2 * i + 1], cond[2 * i]) for i in range(4)]
            quads = [jnp.where(mid, pairs[2 * i + 1], pairs[2 * i]) for i in range(2)]
            K[1 + xl, zb, pl.ds(TILE, SY), :] = jnp.where(top, quads[1], quads[0])

    at_each(sends_x, lambda way: kx_copy(way).start())

    @pl.loop(0, ZB)
    def _(zb):
        for xl in range(SX):
            kys[0, zb, pl.ds(xl, 1), :] = K[1 + xl, zb, pl.ds(TILE, 1), :]
            kys[1, zb, pl.ds(xl, 1), :] = K[1 + xl, zb, pl.ds(TILE + SY - 1, 1), :]

    at_each(sends_y, lambda way: ky_copy(way).start())

    def pack_y(par, way):
        row = TILE if way == 0 else TILE + SY - 1

        @pl.loop(0, ZB)
        def _(zb):
            for xl in range(SX):
                ys[par, way, zb, pl.ds(xl, 1), :] = F[par][1 + xl, zb, pl.ds(row, 1), :]

    def unpack_y(par, side):
        row = TILE - 1 if side == 0 else TILE + SY

        @pl.loop(0, ZB)
        def _(zb):
            for xl in range(SX):
                F[par][1 + xl, zb, pl.ds(row, 1), :] = yr[par, side, zb, pl.ds(xl, 1), :]

    for zb in range(ZB):
        loads[ZB + zb].wait()

    for way in range(2):
        pack_y(0, way)
    at_each(sends_y, lambda way: y_copy(way, 0).start())

    @pl.loop(0, NC)
    def _(c):
        at_each(sends_x, lambda way: x_copy(way, 0, c).start())

    lane = lax.broadcasted_iota(jnp.int32, (SY, LANES), 1)
    last_lane, first_lane = lane == LANES - 1, lane == 0

    @pl.loop(0, SX)
    def _(xl):
        line = [K[1 + xl, zb, pl.ds(TILE, SY), :] for zb in range(ZB)]
        ahead = [pltpu.roll(k, LANES - 1, 1) for k in line] + [jnp.zeros((SY, LANES), jnp.float32)]
        behind = [jnp.zeros((SY, LANES), jnp.float32)] + [pltpu.roll(k, 1, 1) for k in line]
        for zb in range(ZB):
            high = jnp.where(last_lane, ahead[zb + 1], ahead[zb])
            low = jnp.where(first_lane, behind[zb], behind[zb + 1])
            GzH[xl, zb] = face_step * (line[zb] + high)
            GzL[xl, zb] = face_step * (line[zb] + low)

    def x_faces(p):
        @pl.loop(0, ZB)
        def _(zb):
            Gx[p, zb] = face_step * (K[p, zb, pl.ds(TILE, SY), :] + K[p + 1, zb, pl.ds(TILE, SY), :])

    @pl.loop(1, SX)
    def _(p):
        x_faces(p)

    wait_arrivals(meta_copy)
    even = lax.rem(t, 2) == 0
    lin_rows = []
    for q in range(qgroups):
        first, second = metar[2 * q], metar[2 * q + 1]
        first = jnp.where(even, first, pltpu.roll(first, CAP, 1))
        second = jnp.where(even, pltpu.roll(second, CAP, 1), second)
        lin = jnp.where(lane8 < CAP, first, second)
        lin_rows.append(lin)
        gidx_v[pl.ds(q, 1), :] = jnp.maximum(lin[0:1], 0)
    to_smem = pltpu.make_async_copy(gidx_v, gidx_s, idx_sem)
    to_smem.start()

    @pl.loop(0, voxel_blocks // LANES)
    def _(i):
        rows = lax.broadcasted_iota(jnp.int32, (LANES, LANES), 0) + i * LANES
        for q in range(qgroups):
            O[pl.ds(pl.multiple_of(i * LANES, LANES), LANES), q * LANES : (q + 1) * LANES] = one_hot(
                rows == jnp.broadcast_to(lin_rows[q][0:1], (LANES, LANES))
            )

    to_smem.wait()

    at_each(gets_y, lambda way: ky_copy(way).wait_recv())

    @pl.loop(0, ZB)
    def _(zb):
        for xl in range(SX):
            K[1 + xl, zb, pl.ds(TILE - 1, 1), :] = kyr[0, zb, pl.ds(xl, 1), :]
            K[1 + xl, zb, pl.ds(TILE + SY, 1), :] = kyr[1, zb, pl.ds(xl, 1), :]

    @pl.loop(0, SX)
    def _(xl):
        @pl.loop(0, ZB)
        def _(zb):
            Gy[xl, zb, pl.ds(TILE - 1, 1), :] = face_step * (
                K[1 + xl, zb, pl.ds(TILE - 1, 1), :] + K[1 + xl, zb, pl.ds(TILE, 1), :]
            )
            Gy[xl, zb, pl.ds(TILE, SY), :] = face_step * (
                K[1 + xl, zb, pl.ds(TILE, SY), :] + K[1 + xl, zb, pl.ds(TILE + 1, SY), :]
            )

    def split_rows(src):
        @pl.loop(0, n_tool)
        def _(s):
            hi, lo = split_pair(src[s])
            at = pl.ds(pl.multiple_of(s * CAP, CAP), CAP)
            R[at, 0:LANES] = hi
            R[at, LANES : 2 * LANES] = lo

    def scatter(write):
        @pl.loop(0, voxel_blocks // step_rows)
        def _(m):
            at = pl.ds(pl.multiple_of(m * step_rows, step_rows), step_rows)
            got = jnp.dot(
                O[at, :], R[...], preferred_element_type=jnp.float32
            )
            write(at, source_step * (got[:, :LANES] + got[:, LANES:]))

    def to_source(at, rows):
        SRC[at, :] = rows

    def to_weight(at, rows):
        W[at, :] = rows

    def to_rest(at, rows):
        BD[at, :] = rows

    wait_arrivals(msg1_copy)
    split_rows(msg1r)
    scatter(to_source)

    at_each(gets_x, lambda way: kx_copy(way).wait_recv())
    x_faces(0)
    x_faces(SX)

    def add_gains():
        for copy in small[7:]:
            copy.wait()
        for j in range(BEADROWS // TILE):
            @pl.loop(0, TILE)
            def _(i, j=j):
                at = pl.ds(pl.multiple_of(i * LANES, LANES), LANES)
                shell = bead_rows[pl.ds(j * TILE + i, 1), :]
                row, lane = shell // LANES, shell % LANES
                A[:, at] = one_hot(
                    lax.broadcasted_iota(jnp.int32, (BLK, LANES), 0) == jnp.broadcast_to(row, (BLK, LANES))
                )
                here = lax.broadcasted_iota(jnp.int32, (LANES, LANES), 0) == jnp.broadcast_to(lane, (LANES, LANES))
                held = jnp.where(here, jnp.broadcast_to(gain_rows[pl.ds(j * TILE + i, 1), :], (LANES, LANES)), 0.0)
                hi, lo = split_pair(held)
                BT[0:LANES, at] = hi
                BT[LANES : 2 * LANES, at] = lo

            part = lax.dot_general(
                A[...], BT[...], (((1,), (1,)), ((), ())), preferred_element_type=jnp.float32
            )
            if j == 0:
                acc[...] = part
            else:
                acc[...] += part

    def pack_pair(rows, out):
        hi, lo = split_pair(rows)
        XB[:, 0:LANES] = hi
        XB[:, LANES : 2 * LANES] = lo

        def write(d, rows):
            out[pl.ds(d, part_rows // CAP)] = rows

        pack(write)

    def shells_after_first():
        small[6].wait()
        sigma = 1.0 - 0.4 * jnp.tanh(theta0[...])
        rate = base_rate[...] + sigma * (acc[:, :LANES] + acc[:, LANES:])
        outflow = film[...] * (theta0[...] - contact[...])
        theta1[...] = theta0[...] + shell_step * (sigma * rate - outflow)

    lane_t = lax.broadcasted_iota(jnp.int32, (TILE, LANES), 1)
    top_lane, low_lane = lane_t == LANES - 1, lane_t == 0
    no_heat = jnp.zeros((TILE, LANES), jnp.float32)

    def planes(par, y0, first, last, final):
        old, new = F[par], F[1 - par]
        y0 = pl.multiple_of(y0, TILE)
        rows = pl.ds(pl.multiple_of(y0 + TILE, TILE), TILE)
        all_z = range(ZB)

        def temp(p, zb, shift=0):
            return old[p, zb, rows if shift == 0 else pl.ds(y0 + TILE + shift, TILE), :]

        center = [temp(first, zb) for zb in all_z]
        below = [Gx[first - 1, zb, pl.ds(y0, TILE), :] * (center[zb] - temp(first - 1, zb)) for zb in all_z]
        for p in range(first, last):
            xl = p - 1
            ahead = [temp(p + 1, zb) for zb in all_z]
            above = [Gx[p, zb, pl.ds(y0, TILE), :] * (ahead[zb] - center[zb]) for zb in all_z]
            after = [pltpu.roll(now, LANES - 1, 1) for now in center] + [no_heat]
            before = [no_heat] + [pltpu.roll(now, 1, 1) for now in center]
            for zb in all_z:
                now = center[zb]
                z_high = GzH[xl, zb, pl.ds(y0, TILE), :] * (jnp.where(top_lane, after[zb + 1], after[zb]) - now)
                z_low = GzL[xl, zb, pl.ds(y0, TILE), :] * (now - jnp.where(low_lane, before[zb], before[zb + 1]))
                y_high = Gy[xl, zb, rows, :] * (temp(p, zb, 1) - now)
                y_low = Gy[xl, zb, pl.ds(y0 + TILE - 1, TILE), :] * (now - temp(p, zb, -1))
                at = pl.multiple_of((xl * ZB + zb) * SY + y0, TILE)
                total = (above[zb] - below[zb]) + (y_high - y_low) + (z_high - z_low)
                result = now + (total + SRC[pl.ds(at, TILE), :])
                if final:
                    FG[pl.ds(at, TILE), :] = result
                else:
                    new[p, zb, rows, :] = result
            center, below = ahead, above

    def collect(k, d):
        q = d // 2
        lane0 = lax.rem(d, 2) * CAP

        @pl.loop(0, CAP // TILE)
        def _(j):
            for i in range(TILE):
                row = gidx_s[q, lane0 + j * TILE + i]
                backs[k, d, pl.ds(pl.multiple_of(j * TILE, TILE) + i, 1), :] = FG[pl.ds(row, 1), :]

    def collect_and_send(k, first, last):
        @pl.loop(first, last)
        def _(off):
            d = partner(off)
            collect(k, d)
            back_copy[k](d, t).start()

    def next_source(c):
        @pl.loop(0, SX)
        def _(xl):
            for zb in range(ZB):
                at = pl.ds(pl.multiple_of((xl * ZB + zb) * SY + c * CY, TILE), CY)
                now = FA[1 + xl, zb, pl.ds(pl.multiple_of(TILE + c * CY, TILE), CY), :]
                FG[at, :] = now
                SRC[at, :] = BD[at, :] - W[at, :] * now

    def sweep(par, started=True, fresh=None, final=False):
        new = 1 - par

        @pl.loop(0, NC)
        def _(k):
            c = jnp.where(k == 0, 0, jnp.where(k == 1, NC - 1, k - 1))
            first, last = k == 0, k == 1

            @pl.when(first)
            def _():
                @pl.when(has_down)
                def _():
                    y_copy(1, par).wait_recv()

                unpack_y(par, 0)

            @pl.when(last)
            def _():
                @pl.when(has_up)
                def _():
                    y_copy(0, par).wait_recv()

                unpack_y(par, 1)

            if fresh is not None:
                @pl.when(fresh)
                def _():
                    next_source(c)

            at_each(gets_x, lambda way: x_copy(way, par, c).wait_recv())

            @pl.when(started)
            def _():
                at_each(sends_x, lambda way: x_copy(way, new, c).wait_send())

            @pl.loop(0, CY // TILE)
            def _(i):
                planes(par, c * CY + i * TILE, 1, 2, final)
                planes(par, c * CY + i * TILE, SX, SX + 1, final)

            if not final:
                at_each(sends_x, lambda way: x_copy(way, new, c).start())

            @pl.loop(0, CY // TILE)
            def _(i):
                planes(par, c * CY + i * TILE, 2, SX, final)

            def send_y(way):
                @pl.when(started)
                def _():
                    y_copy(way, new).wait_send()

                if not final:
                    pack_y(new, way)
                    y_copy(way, new).start()

            @pl.when(first & has_down)
            def _():
                send_y(0)

            @pl.when(last & has_up)
            def _():
                send_y(1)

    @pl.loop(0, STEPS * SWEEPS // 2 - 1)
    def _(pair):
        sweep(0, started=pair > 0, fresh=pair == 2)

        @pl.when(pair == 0)
        def _():
            pack_pair(film[...], msgWs)
            send_all(msgW_copy, 1, n_tool)
            msgWr[t] = msgWs[t]
            add_gains()

        @pl.when(pair == 1)
        def _():
            wait_arrivals(msgW_copy)
            split_rows(msgWr)
            scatter(to_weight)

        @pl.when(pair == 2)
        def _():
            collect_and_send(0, 1, n_tool // 3 + 1)
            collect(0, t)

        sweep(1)

        @pl.when(pair == 2)
        def _():
            collect_and_send(0, n_tool // 3 + 1, 2 * n_tool // 3 + 1)

        @pl.when(pair == 1)
        def _():
            wait_arrivals(msgB_copy)
            split_rows(msgBr)
            scatter(to_rest)

        @pl.when(pair == 0)
        def _():
            shells_after_first()
            pack_pair(film[...] * theta1[...], msgBs)
            send_all(msgB_copy, 1, n_tool)
            msgBr[t] = msgBs[t]

    sweep(0)
    collect_and_send(0, 2 * n_tool // 3 + 1, n_tool)
    sweep(1, final=True)

    stores = [
        pltpu.make_async_copy(
            FG.at[pl.ds((xl * ZB + zb) * SY, SY), :],
            tool_out.at[xl, :, pl.ds(zb * LANES, LANES)],
            out_sem.at[xl, zb],
        )
        for xl in range(SX)
        for zb in range(ZB)
    ]
    collect_and_send(1, 1, n_tool)
    collect(1, t)
    for copy in stores:
        copy.start()

    def contact_of(k):
        backr[k, t] = backs[k, t]
        wait_arrivals(back_copy[k])
        split_rows(backr.at[k])
        got = jnp.dot(PT[...], R[...], preferred_element_type=jnp.float32)
        return got[:, :LANES] + got[:, LANES:]

    flux = film[...] * (contact_of(0) - theta1[...])
    sigma = 1.0 - 0.4 * jnp.tanh(theta1[...])
    rate = base_rate[...] + sigma * (acc[:, :LANES] + acc[:, LANES:])
    shell_end[...] = theta1[...] + shell_step * (flux + sigma * rate)
    stores.append(pltpu.make_async_copy(shell_end, shell_out, end_sem.at[0]))
    stores[-1].start()
    contact_end[...] = contact_of(1)
    stores.append(pltpu.make_async_copy(contact_end, contact_out, end_sem.at[1]))
    stores[-1].start()

    wait_sends(meta_copy)
    wait_sends(msg1_copy)
    wait_sends(msgW_copy)
    wait_sends(msgB_copy)
    wait_sends(back_copy[0])
    wait_sends(back_copy[1])
    at_each(sends_x, lambda way: kx_copy(way).wait_send())
    at_each(sends_y, lambda way: ky_copy(way).wait_send())

    @pl.loop(0, NC)
    def _(c):
        at_each(sends_x, lambda way: x_copy(way, 1, c).wait_send())

    at_each(sends_y, lambda way: y_copy(way, 1).wait_send())

    for copy in stores:
        copy.wait()


MESH = pl.DeviceIdType.MESH


def on_device(n_tool, n_blank, tool_temp, material, conductivity, shell_temp, base_rate, film, contact_temp, pair_slab, pair_block, bead_ids, bead_gain):
    SX, SY, SZ = tool_temp.shape
    ZB = SZ // LANES
    NC = CHUNKS
    BLK = shell_temp.shape[0]
    beadrows = bead_ids.shape[0] // LANES
    slots = n_tool * CAP
    voxel_blocks = SX * SY * ZB
    f32, bf16, i32 = jnp.float32, jnp.bfloat16, jnp.int32
    V = pltpu.VMEM
    dma = pltpu.SemaphoreType.DMA
    scratch = [
        pltpu.SMEM(conductivity.shape, f32),
        V((BLK, LANES), f32),
        V((BLK, LANES), f32),
        V((BLK, LANES), f32),
        V((BLK, LANES), f32),
        V((BLK // LANES, LANES), i32),
        V((BLK // LANES, LANES), i32),
        V((beadrows, LANES), i32),
        V((beadrows, LANES), f32),
        V((BLK, LANES), f32),
        V((BLK, LANES), f32),
        V((SX + 2, ZB, SY + 2 * TILE, LANES), f32),
        V((SX + 2, ZB, SY + 2 * TILE, LANES), f32),
        V((SX + 2, ZB, SY + 2 * TILE, LANES), f32),
        V((SX, ZB, SY, LANES), i32),
        V((SX + 1, ZB, SY, LANES), f32),
        V((SX, ZB, SY + TILE, LANES), f32),
        V((SX, ZB, SY, LANES), f32),
        V((SX, ZB, SY, LANES), f32),
        V((voxel_blocks, LANES), f32),
        V((voxel_blocks, LANES), f32),
        V((voxel_blocks, LANES), f32),
        V((voxel_blocks, LANES), f32),
        V((voxel_blocks, slots), bf16),
        V((slots, BLK), bf16),
        V((BLK, slots), bf16),
        V((BLK, 2 * LANES), bf16),
        V((slots, 2 * LANES), bf16),
        V((BLK, TILE * LANES), bf16),
        V((2 * LANES, TILE * LANES), bf16),
        V((BLK, 2 * LANES), f32),
        V((BLK, LANES), i32),
        V((BLK, LANES), i32),
        V((slots // LANES, TILE, LANES), i32),
        V((n_tool, TILE, LANES), i32),
        V((slots // LANES, LANES), i32),
        pltpu.SMEM((slots // LANES, LANES), i32),
        V((2, 2, ZB, SX, LANES), f32),
        V((2, 2, ZB, SX, LANES), f32),
        V((2, ZB, SX, LANES), f32),
        V((2, ZB, SX, LANES), f32),
        V((n_tool, CAP, LANES), f32),
        V((n_tool, CAP, LANES), f32),
        V((n_tool, CAP, LANES), f32),
        V((n_tool, CAP, LANES), f32),
        V((n_tool, CAP, LANES), f32),
        V((n_tool, CAP, LANES), f32),
        V((STEPS, n_tool, CAP, LANES), f32),
        V((STEPS, n_tool, CAP, LANES), f32),
        V((BLK, LANES), f32),
        dma((9,)),
        dma((2, ZB)),
        dma((SX, ZB)),
        dma((2,)),
        dma,
        dma((2, 2, NC)),
        dma((2, 2, NC)),
        dma((2, 2)),
        dma((2, 2)),
        dma((2, 2)),
        dma((2, 2)),
        dma((n_tool,)),
        dma((n_tool,)),
        dma((n_tool,)),
        dma((n_tool,)),
        dma((n_tool,)),
        dma((n_tool,)),
        dma((n_tool,)),
        dma((n_tool,)),
        dma((STEPS, n_tool)),
        dma((STEPS, n_tool)),
    ]
    far = pl.BlockSpec(memory_space=pl.ANY)
    results = pl.pallas_call(
        functools.partial(kernel, (n_tool, n_blank, SX, SY, ZB, BLK, beadrows)),
        out_shape=(
            jax.ShapeDtypeStruct(tool_temp.shape, f32),
            jax.ShapeDtypeStruct(shell_temp.shape, f32),
            jax.ShapeDtypeStruct(shell_temp.shape, f32),
        ),
        in_specs=[far] * 11,
        out_specs=(far,) * 3,
        scratch_shapes=scratch,
        compiler_params=pltpu.CompilerParams(
            collective_id=0, has_side_effects=True, vmem_limit_bytes=60 * 2**20
        ),
    )(
        tool_temp,
        material,
        conductivity,
        shell_temp,
        base_rate,
        film,
        contact_temp,
        pair_slab.reshape(BLK // LANES, LANES),
        pair_block.reshape(BLK // LANES, LANES),
        bead_ids.reshape(beadrows, LANES),
        bead_gain.reshape(beadrows, LANES),
    )

    return pl.pallas_call(
        write_out,
        out_shape=tuple(jax.ShapeDtypeStruct(r.shape, r.dtype) for r in results),
        in_specs=[far] * 3,
        out_specs=(far,) * 3,
        scratch_shapes=[V(r.shape, f32) for r in results] + [dma((SX + 2,)), dma((SX + 2,))],
        compiler_params=pltpu.CompilerParams(vmem_limit_bytes=60 * 2**20),
    )(*results)


def write_out(tool_in, shell_in, contact_in, tool_out, shell_out, contact_out, tool_held, shell_held, contact_held, in_sems, out_sems):
    n = tool_in.shape[0]
    parts = [(tool_in.at[i], tool_held.at[i], tool_out.at[i]) for i in range(n)]
    parts += [(shell_in, shell_held, shell_out), (contact_in, contact_held, contact_out)]
    reads = [pltpu.make_async_copy(src, held, in_sems.at[i]) for i, (src, held, _) in enumerate(parts)]
    writes = [pltpu.make_async_copy(held, dst, out_sems.at[i]) for i, (_, held, dst) in enumerate(parts)]
    for copy in reads:
        copy.start()
    for read, write in zip(reads, writes):
        read.wait()
        write.start()
    for copy in writes:
        copy.wait()


def solution(mesh):
    placed = (
        P("tool", "blank", None),
        P("tool", "blank", None),
        P(),
        P(("blank", "tool"), None),
        P(("blank", "tool"), None),
        P(("blank", "tool"), None),
        P(("blank", "tool"), None),
        P(("blank", "tool"), None),
        P(("blank", "tool")),
        P(("blank", "tool")),
        P(("blank", "tool")),
    )
    return jax.shard_map(
        functools.partial(on_device, mesh.shape["tool"], mesh.shape["blank"]),
        mesh=mesh,
        in_specs=placed,
        out_specs=(
            P("tool", "blank", None),
            P(("blank", "tool"), None),
            P(("blank", "tool"), None),
        ),
        check_vma=False,
    )
```
